32 devices in a mesh: grp: 2 (over core), mer: 4 (over z), sub: 4 (over y, x).
Axes of the slice: x: 2, y: 2, z: 4, core: 2. Of those that a mesh axis runs over, the one named last changes fastest.
Arguments:
- field: float32 [2, 256, 16384], P('grp', 'sub', 'mer'), may hold values from -6 to 6
- previous: float32 [2, 256, 16384], P('grp', 'sub', 'mer'), may hold values from -6 to 6
- stiff: float32 [2, 128, 128], P('grp'), as said below
- synth: float32 [2, 256, 256], P('grp', None, 'sub'), may hold values from -0.5 to 0.5
- owner: int32 [2, 1024, 1], P('grp', 'mer'), may hold values from 0 to 3; in each aligned block of 256 rows (0 to 255, 256 to 511, ..., all dimensions but the last counted through in order) at most 128 rows name the same one
- face: int32 [2, 1024], P('grp', 'mer'), may hold values from 0 to 255
- weight: float32 [2, 1024], P('grp', 'mer'), may hold values from 0.3 to 1.7
Outputs:
- latest: float32 [2, 256, 16384], P('grp', 'sub', 'mer')
- prior: float32 [2, 256, 16384], P('grp', 'sub', 'mer')
The draws below stay inside these ranges and needn't reach their ends.
Inputs may be any that keep to these rules, and one draw needn't show every extreme that they name: Among the 256 interface points of one domain, at most 128 name the same owner, and in some domains exactly 128 do. `stiff`: each model's element matrix is symmetric.
All inputs are finite; a program needn't handle non-finite values.
Results may differ from the reference program's by a relative error of at most 0.0001.
Values sent between devices are 32-bit elements; how exact they have to be, the bound alone decides.
No kernel may reach another device: no remote copies, remote signals or barrier semaphores. Data moves between devices by JAX's collectives and lax.ppermute only.
A program may use at most 64 MiB of HBM per device.

```python
import math
import jax
import jax.numpy as jnp
import numpy as np
from jax import lax

CH = 256
PTS = 4096
EP = 128
IFC = 256
ITERS = 2
POINTS = 16384
CAP = 128
N_MER = 4


def draw_stiff(key, part):
    random_part = jax.random.normal(key, (2, EP, EP), jnp.float32)
    random_part = random_part * (0.25 / EP ** 0.5)
    symmetric = (random_part + jnp.swapaxes(random_part, 1, 2)) / 2.0 ** 0.5
    return (jnp.eye(EP, dtype=jnp.float32)[None, :, :] + symmetric).astype(jnp.float32)


def touch_ends(values, own_key, low, top_value):
    place = [jax.random.randint(jax.random.fold_in(own_key, axis), (), 0, length) for axis, length in enumerate(values.shape)]
    longest = values.shape.index(max(values.shape))
    neighbour = place[:longest] + [(place[longest] + 1) % values.shape[longest]] + place[longest + 1:]
    return values.at[tuple(place)].set(low).at[tuple(neighbour)].set(top_value)


def with_spikes(drawn, key, source, target, parts, factor):
    owner, partner = [(jnp.arange(drawn.shape[position]) // (drawn.shape[position] // parts)).reshape([-1 if axis == position else 1 for axis in range(drawn.ndim)]) for position in (source, target)]
    chosen = jax.random.permutation(key, parts)[partner]
    strong = (owner == chosen) | (owner == (partner + parts // 2) % parts)
    return jnp.where(strong, factor * drawn, drawn)


def level_of(own_key, shape, cuts, low, top_value):
    level = 1.0
    for axis_at, parts in cuts:
        steps = jax.random.uniform(jax.random.fold_in(jax.random.fold_in(own_key, 6), axis_at), (parts,), jnp.float32, low / len(cuts), top_value / len(cuts))
        level = level * jnp.repeat(jnp.exp(steps), shape[axis_at] // parts).reshape((-1,) + (1,) * (len(shape) - 1 - axis_at))
    return level


def deal_out(rng, own, number, rows, number_of, top, reach, lean):
    order = jax.random.permutation(rng, number_of)
    crowded, ordinary = portions_of(number_of, rows * top, reach, lean, True), portions_of(number_of, rows * top, reach, lean, False)
    places = jnp.arange(number_of)

    def named(sizes, rotation):
        used = int((sizes > 0).sum())
        fixed = max(1, used // 4)
        moved = fixed + (places - fixed + rotation * (used - fixed)) % max(1, number_of - fixed)
        return jnp.zeros((number_of,), jnp.int32).at[order[jnp.where(places < fixed, places, moved)]].set(jnp.asarray(sizes, jnp.int32))

    sizes = jnp.where(number % 4 == 0, named(crowded, number // 4), named(ordinary, number - number // 4 - 1))
    mixed = jax.random.permutation(jax.random.fold_in(own, 3), number_of)
    source_of, taker = mixed[0:number_of // 2 * 2:2], mixed[1:number_of // 2 * 2:2]
    slack = jnp.minimum(sizes[source_of] - 1, reach - sizes[taker]) // 2
    slack = jnp.where((source_of == order[0]) | (taker == order[0]) | (sizes[taker] == 0), 0, jnp.maximum(slack, 0))
    moved = jax.random.randint(jax.random.fold_in(own, 4), (number_of // 2,), 0, 1 << 20) % (slack + 1)
    sizes = sizes.at[source_of].add(-moved).at[taker].add(moved)
    items = jnp.searchsorted(jnp.cumsum(sizes), jnp.arange(rows * top), side="right").astype(jnp.int32)
    grid = items.reshape(top, rows).T
    grid = grid[jax.random.permutation(jax.random.fold_in(own, 1), rows)]
    rotation = jax.random.randint(jax.random.fold_in(own, 2), (rows, 1), 0, top)
    return jnp.take_along_axis(grid, (jnp.arange(top)[None, :] + rotation) % top, axis=1)


def portions_of(number_of, total, most, lean, full):
    weights = [(1 << 20) // math.isqrt(grade ** lean) + 1 for grade in range(1, number_of + 1)]
    largest = most if full else min(most, max(-(-total // number_of), total * weights[0] // sum(weights)))
    least = 1 if total - largest >= number_of - 1 else 0
    counts, spare = [largest] + [least] * (number_of - 1), total - largest - least * (number_of - 1)
    while spare > 0:
        candidates = [i for i in range(1, number_of) if counts[i] < largest] or [i for i in range(1, number_of) if counts[i] < most]
        whole, left = sum([weights[i] for i in candidates]), spare
        for i in candidates:
            addition = min(most - counts[i], max(1, left * weights[i] // whole), spare)
            counts[i] = counts[i] + addition
            spare = spare - addition
    return np.array(counts)


def gaussian(rng, shape, spread, most, cuts=(), kind=jnp.bfloat16):
    loudness = level_of(rng, shape, cuts, -0.22, 0.18) if cuts else 1.0
    entries = jax.random.normal(rng, shape, jnp.float32) * spread * loudness
    return jnp.minimum(jnp.maximum(entries, -most), most).astype(kind)


def gaussian_with(stream_key, extent, width, limit, split, heavy, kind=jnp.bfloat16):
    drawn = width * jax.random.normal(stream_key, extent, jnp.float32)
    if split:
        drawn = drawn * level_of(stream_key, extent, split, -0.22, 0.18)
    return jnp.clip(with_spikes(drawn, jax.random.fold_in(stream_key, 3), *heavy), -limit, limit).astype(kind)


def setup_inputs(seed: int = 0) -> dict:
    key_list = jax.random.split(jax.random.key(seed), 8)
    field = gaussian(key_list[0], (2, CH, POINTS), 1.0, 6.0, ((0, 2), (1, 4), (2, 4)), jnp.float32)
    previous = gaussian(key_list[1], (2, CH, POINTS), 1.0, 6.0, ((0, 2), (1, 4), (2, 4)), jnp.float32)
    stiff = draw_stiff(jax.random.fold_in(key_list[7], 71), 0)
    synth = gaussian_with(key_list[3], (2, CH, CH), CH ** -0.5, 0.5, ((0, 2), (2, 4)), (2, 1, 4, 2.0), jnp.float32)
    owner_keys = jax.random.split(jax.random.fold_in(key_list[4], 1), 2 * (POINTS * IFC // PTS) // IFC)
    owner_turns = jax.random.permutation(jax.random.fold_in(key_list[4], 3), 2 * (POINTS * IFC // PTS) // IFC)
    owner = jax.vmap(lambda own, number: deal_out(jax.random.fold_in(key_list[4], 2), own, number, IFC, N_MER, 1, CAP, 2))(owner_keys, owner_turns).reshape((2, POINTS * IFC // PTS, 1))
    face = touch_ends(jax.random.randint(key_list[5], (2, POINTS * IFC // PTS), 0, IFC), jax.random.fold_in(key_list[5], 1), 0, IFC - 1).astype(jnp.int32)
    weight = jnp.clip(0.3 + 1.40000004 * jax.random.uniform(key_list[6], (2, POINTS * IFC // PTS), jnp.float32) ** level_of(key_list[6], (2, POINTS * IFC // PTS), ((0, 2), (1, 4)), -0.2, 0.2), 0.3, 1.7)
    return dict(field=field, previous=previous, stiff=stiff, synth=synth, owner=owner, face=face, weight=weight)


DT2 = 0.5
KAPPA = 0.5


def advance(state, older, stiff, synth, owner, face, weight):
    total = state.shape[2]
    padded = jnp.pad(state, ((0, 0), (0, 0), (1, 1)))
    lap = 2.0 * state - padded[:, :, 2:] - padded[:, :, :-2]
    blocks = state.reshape(2, CH, total // EP, EP)
    stiffened = jnp.einsum("gcne,gef->gcnf", blocks, stiff, precision=lax.Precision.HIGHEST).reshape(state.shape)
    shards = state.reshape(2, CH, N_MER, PTS)
    surface = shards[:, :, :, :IFC].reshape(2, CH, N_MER * IFC)
    traces = jnp.einsum("goc,gci->goi", synth, surface, precision=lax.Precision.HIGHEST) * weight[:, None, :]
    forces = []
    for group in range(2):
        target = (owner[group, :, 0] * IFC + face[group]).astype(jnp.int32)
        summed = jax.ops.segment_sum(traces[group].T, target, num_segments=N_MER * IFC)
        forces.append(summed.T)
    incoming = jnp.stack([forces[1], forces[0]]).reshape(2, CH, N_MER, IFC)
    forcing = jnp.pad(incoming, ((0, 0), (0, 0), (0, 0), (0, PTS - IFC))).reshape(state.shape)
    newer = 2.0 * state - older + DT2 * (forcing - stiffened - KAPPA * lap)
    return newer, state


def reference(field, previous, stiff, synth, owner, face, weight):
    state, older = field, previous
    for step in range(ITERS):
        state, older = advance(state, older, stiff, synth, owner, face, weight)
    return state, older
```

```python
import functools

import jax
import jax.numpy as jnp
from jax import lax
from jax.experimental import pallas as pl
from jax.experimental.pallas import tpu as pltpu
from jax.sharding import PartitionSpec as P

F32 = jnp.float32
BF16 = jnp.bfloat16
HIGHEST = lax.Precision.HIGHEST
VMEM_BYTES = 48 * 2**20
LABELS = 8
NT = (((1,), (1,)), ((), ()))


def split(x):
    high = x.astype(BF16)
    return high, (x - high.astype(F32)).astype(BF16)


def dot(a, b):
    return jnp.dot(a, b, preferred_element_type=F32)


def dot_nt(a, b):
    return lax.dot_general(a, b, NT, preferred_element_type=F32)


def times_matrix(x, matrix):
    rows, size = x.shape[0], matrix.shape[0]
    count = x.shape[1] // size
    tall = x if count == 1 else jnp.concatenate([x[:, e * size : (e + 1) * size] for e in range(count)], axis=0)
    high, low = split(tall)
    mh, ml = split(matrix)
    out = dot(high, mh) + (dot(low, mh) + dot(high, ml))
    if count == 1:
        return out
    return jnp.concatenate([out[e * rows : (e + 1) * rows] for e in range(count)], axis=1)


def neighbours(x):
    width = x.shape[1]
    col = lax.broadcasted_iota(jnp.int32, x.shape, 1)
    lower = jnp.where(col == 0, 0.0, pltpu.roll(x, 1, 1))
    higher = jnp.where(col == width - 1, 0.0, pltpu.roll(x, width - 1, 1))
    return lower + higher


def update(x, matrix):
    return 1.5 * x - 0.5 * times_matrix(x, matrix) + 0.25 * neighbours(x)


def strip_kernel(n, field_ref, fend_ref, prev_ref, pend_ref, stiff_ref, owner_ref, face_ref, weight_ref, *outs):
    me = lax.axis_index("mer")
    iface = owner_ref.shape[1]
    cap = outs[0].shape[1] - iface
    rows = field_ref.shape[1]
    matrix = stiff_ref[0]
    wide = field_ref[0]
    strip = wide[:, :iface]
    nxt = (1.5 * strip - prev_ref[0] - 0.5 * times_matrix(strip, matrix)) + 0.25 * neighbours(wide)[:, :iface]
    fend = fend_ref[0]
    size = fend.shape[1]
    nend = update(fend, matrix) - pend_ref[0]
    owners = owner_ref[...]
    weights = weight_ref[...]
    faces = face_ref[...].astype(F32)
    target = owners.astype(F32) * float(iface) + faces
    count = -(-n // 8) * 8
    dest = lax.broadcasted_iota(jnp.int32, (count, iface), 0) ^ me
    match = jnp.where(owners == dest, 1.0, 0.0)
    before = lax.broadcasted_iota(jnp.int32, (iface, iface), 0) < lax.broadcasted_iota(jnp.int32, (iface, iface), 1)
    rank = dot(match.astype(BF16), jnp.where(before, 1.0, 0.0).astype(BF16))
    slots = jnp.where(match > 0.5, rank, -1.0)
    nh, nl = split(nxt * weights)
    fh, fl = split(jnp.concatenate([faces + 1.0, jnp.zeros((15, iface), F32)], axis=0))
    lhs = jnp.concatenate([nh, nl, fh, fl], axis=0)
    place = lax.broadcasted_iota(jnp.int32, (cap, iface), 0).astype(F32)
    edges = [
        jnp.transpose(fend)[size - 1 : size, :],
        jnp.transpose(nend)[size - 1 : size, :],
        jnp.transpose(nxt[:, :size])[0:1, :],
        jnp.transpose(strip[:, :size])[0:1, :],
    ]
    for k in range(n):
        out = outs[k]
        chosen = jnp.where(slots[k : k + 1, :] == place, 1.0, 0.0).astype(BF16)
        got = dot_nt(lhs, chosen)
        out[0:rows, 0:iface] = strip
        out[0:rows, iface:] = got[0:rows] + got[rows : 2 * rows]
        out[rows:, :] = jnp.zeros((LABELS, iface + cap), F32)
        out[rows : rows + 1, 0:iface] = target
        out[rows + 1 : rows + 2, 0:iface] = weights
        out[rows : rows + 1, iface:] = got[2 * rows : 2 * rows + 1] + got[2 * rows + 16 : 2 * rows + 17] - 1.0
        for e, edge in enumerate(edges):
            out[rows + 2 + e : rows + 3 + e, 0:rows] = edge


def bulk_kernel(field_ref, prev_ref, stiff_ref, latest_ref, prior_ref):
    matrix = stiff_ref[0]
    state = field_ref[0]
    first = update(state, matrix) - prev_ref[0]
    prior_ref[0] = first
    latest_ref[0] = update(first, matrix) - state


def synth_kernel(n_sub, *refs):
    own, other, full, prod_ref, double_ref = refs[0], refs[n_sub], refs[-1], refs[-3], refs[-2]
    sub = lax.axis_index("sub")
    rows = own.shape[0]
    for k in range(n_sub):
        start = pl.multiple_of((sub ^ k) * rows, rows)
        full[pl.ds(start, rows), :] = refs[k][...]

    def packed(x):
        high = x.astype(BF16).astype(F32)
        low = x - high
        return jnp.transpose(jnp.concatenate([high, low, high], axis=0)).astype(BF16)

    prod_ref[...] = packed(own[...])
    twice = 0.5 * jnp.dot(other[...], full[...], precision=HIGHEST, preferred_element_type=F32)
    double_ref[...] = packed(twice)


def message(refs, k):
    return refs[k] if len(refs) > 1 else refs[0].at[k]


def loop(n, body, init):
    if n <= 8:
        for k in range(n):
            init = body(k, init)
        return init
    return lax.fori_loop(0, n, body, init)


def hits(target, base, iface):
    return jnp.where(target - base == lax.broadcasted_iota(jnp.int32, (iface, iface), 0).astype(F32), 1.0, 0.0).astype(BF16)


def domain_base(me, k, iface):
    return ((me ^ k) * iface).astype(F32)


def weighted(ref, x, rows, iface):
    return jnp.concatenate(split(x * ref[rows + 1 : rows + 2, 0:iface]), axis=0)


def gather_kernel(n, iface, rows, *refs):
    msgs, (all_ref, edge_ref, ext_ref) = refs[:-4], refs[-4:-1]
    store = refs[-1]
    me = lax.axis_index("mer")
    edge_ref[...] = jnp.zeros(edge_ref.shape, F32)
    beyond = ((me + 1) * iface).astype(F32)

    def one(k, ext):
        ref = message(msgs, k)
        both = weighted(ref, ref[0:rows, 0:iface], rows, iface)
        store[k] = both
        target = ref[rows : rows + 1, 0:iface]
        mask = jnp.broadcast_to(jnp.where(target == beyond, 1.0, 0.0), (16, iface)).astype(BF16)
        ext = ext + dot_nt(mask, both[:rows]) + dot_nt(mask, both[rows:])
        left = jnp.where((me ^ k) == me - 1, 1.0, 0.0)
        right = jnp.where((me ^ k) == me + 1, 1.0, 0.0)
        edge_ref[0:1, 0:rows] += left * ref[rows + 2 : rows + 3, 0:rows]
        edge_ref[1:2, 0:rows] += left * ref[rows + 3 : rows + 4, 0:rows]
        edge_ref[2:3, 0:rows] += right * ref[rows + 5 : rows + 6, 0:rows]
        edge_ref[3:4, 0:rows] += right * ref[rows + 4 : rows + 5, 0:rows]
        return ext

    ext_ref[...] = loop(n, one, jnp.zeros((16, rows), F32))
    own = message(msgs, 0)
    has_left = jnp.where(me > 0, 0.25, 0.0)
    has_right = jnp.where(me < n - 1, 0.25, 0.0)
    edge_ref[1:2, 0:rows] += has_left * own[rows + 5 : rows + 6, 0:rows]
    edge_ref[3:4, 0:rows] += has_right * own[rows + 2 : rows + 3, 0:rows]

    def onto(j, carry):
        base = domain_base(me, j, iface)

        def add(k, total):
            target = message(msgs, k)[rows : rows + 1, 0:iface]
            return total + dot_nt(store[k], hits(target, base, iface))

        total = loop(n, add, jnp.zeros((2 * rows, iface), F32))
        all_ref[j] = total[:rows] + total[rows:]
        return carry

    loop(n, onto, 0)


def compact_kernel(n, iface, rows, *refs):
    msgs, (out_ref,) = refs[:-4], refs[-4:-3]
    lasts, values, marks = refs[-3:]
    me = lax.axis_index("mer")
    cap = msgs[0].shape[-1] - iface
    base = (me * iface).astype(F32)
    lasts[...] = jnp.zeros(lasts.shape, F32)
    values[...] = jnp.zeros(values.shape, F32)
    marks[...] = jnp.zeros(marks.shape, F32)
    face = lax.broadcasted_iota(jnp.int32, (iface, cap), 0).astype(F32)

    def keep(k, carry):
        lasts[pl.ds((me ^ k) + 1, 1), :] = message(msgs, k)[rows + 2 : rows + 3, 0:rows]
        return carry

    loop(n, keep, 0)

    def one(k, total):
        ref = message(msgs, k)
        both = jnp.concatenate(split(ref[0:rows, iface:]), axis=0)
        here = jnp.where(ref[rows : rows + 1, iface:] == face, 1.0, 0.0).astype(BF16)
        values[pl.ds(k, 1), :] = lasts[pl.ds(me ^ k, 1), :]
        target = ref[rows : rows + 1, 0:1] - base
        weight = 0.25 * ref[rows + 1 : rows + 2, 0:1]
        line = lax.broadcasted_iota(jnp.int32, (1, iface), 1).astype(F32)
        marks[pl.ds(k, 1), :] = jnp.where(target == line, weight, 0.0)
        return total + dot_nt(both, here)

    total = loop(n, one, jnp.zeros((2 * rows, iface), F32))
    first = jnp.dot(jnp.transpose(values[...]), marks[...], precision=HIGHEST, preferred_element_type=F32)
    out_ref[...] = total[:rows] + total[rows:] + first


def share_kernel(n, n_sub, iface, rows, *refs):
    outs = refs[-n_sub:]
    zown_ref, zother_ref, ext_ref, compact_ref, prod_ref, double_ref, synth_ref = refs[-n_sub - 7 : -n_sub]
    msgs = refs[: -n_sub - 7]
    me = lax.axis_index("mer")
    sub = lax.axis_index("sub")
    base = (me * iface).astype(F32)

    def add(k, total):
        ref = message(msgs, k)
        both = weighted(ref, zother_ref[k], rows, iface)
        return total + dot_nt(both, hits(ref[rows : rows + 1, 0:iface], base, iface))

    total = loop(n, add, jnp.zeros((2 * rows, iface), F32))

    def tall(x):
        high, low = split(x)
        return jnp.concatenate([high, high, low], axis=0)

    y0, y1, y2 = tall(zown_ref[0]), tall(compact_ref[...]), tall(total[:rows] + total[rows:])
    ext = jnp.dot(ext_ref[0:8], synth_ref[...], precision=HIGHEST, preferred_element_type=F32)
    for k in range(n_sub):
        start = pl.multiple_of((sub ^ k) * rows, rows)
        prod = prod_ref[pl.ds(start, rows), :]
        outs[k][0:rows, 0:iface] = dot(prod, y0)
        outs[k][0:rows, iface:] = dot(prod, y1) + dot(double_ref[pl.ds(start, rows), :], y2)
        outs[k][rows:, 0 : ext.shape[1]] = ext


def patch_kernel(n_sub, iface, rows, *refs):
    parts = refs[:n_sub]
    edge_ref, stiff_ref, latest_in, prior_in, latest_ref, prior_ref, turned = refs[n_sub:]
    sub = lax.axis_index("sub")
    matrix = stiff_ref[0]
    size = matrix.shape[0]
    width = latest_ref.shape[2]
    edges = jnp.transpose(edge_ref[...])[0:rows, :]

    @pl.when(pl.program_id(0) == 0)
    def _():
        force = functools.reduce(lambda a, b: a + b, [p[0:rows, :] for p in parts])
        col = lax.broadcasted_iota(jnp.int32, (rows, iface), 1)
        delta = 0.5 * force[:, :iface] + jnp.where(col == 0, 0.25 * edges[:, 0:1], 0.0)
        change = update(delta, matrix) + 0.5 * force[:, iface:] + jnp.where(col == 0, 0.25 * edges[:, 1:2], 0.0)
        prior_ref[0, :, 0:iface] = prior_in[0, :, 0:iface] + delta
        prior_ref[0, :, iface:] = prior_in[0, :, iface:]
        latest_ref[0, :, 0:iface] = latest_in[0, :, 0:iface] + change
        rest = latest_in[0, :, iface:]
        col = lax.broadcasted_iota(jnp.int32, rest.shape, 1)
        latest_ref[0, :, iface:] = rest + jnp.where(col == 0, 0.25 * delta[:, iface - 1 : iface], 0.0)

    @pl.when(pl.program_id(0) == 1)
    def _():
        ext = functools.reduce(lambda a, b: a + b, [p[rows:, 0:turned.shape[0]] for p in parts])
        turned[...] = jnp.transpose(ext)
        start = pl.multiple_of(sub * rows, rows)
        beyond = edges[:, 3:4] + 0.5 * turned[pl.ds(start, rows), 0:1]
        col = lax.broadcasted_iota(jnp.int32, (rows, size), 1)
        delta = jnp.where(col == size - 1, 0.25 * edges[:, 2:3], 0.0)
        change = update(delta, matrix) + jnp.where(col == size - 1, 0.25 * beyond, 0.0)
        cut = width - size
        prior_ref[0, :, :cut] = prior_in[0, :, :cut]
        latest_ref[0, :, :cut] = latest_in[0, :, :cut]
        prior_ref[0, :, cut:] = prior_in[0, :, cut:] + delta
        latest_ref[0, :, cut:] = latest_in[0, :, cut:] + change


def call(kernel, outs, cost=None, **more):
    params = pltpu.CompilerParams(vmem_limit_bytes=VMEM_BYTES)
    estimate = None if cost is None else pl.CostEstimate(flops=cost[0], bytes_accessed=cost[1], transcendentals=0)
    return pl.pallas_call(kernel, out_shape=outs, compiler_params=params, cost_estimate=estimate, **more)


def shape(*dims, dtype=F32):
    return jax.ShapeDtypeStruct(dims, dtype)


def body(field, previous, stiff, synth, owner, face, weight):
    n, n_sub = lax.axis_size("mer"), lax.axis_size("sub")
    _, rows, points = field.shape
    size = stiff.shape[1]
    iface = face.shape[1]
    chans = synth.shape[1]
    most = 2 * iface // n
    cap = -(-most // 128) * 128
    block = pltpu.VMEM
    whole = pl.BlockSpec(memory_space=block)
    table = jnp.transpose(synth[0])

    lead = pl.BlockSpec((1, rows, iface + size), lambda i: (0, 0, 0))
    strip = pl.BlockSpec((1, rows, iface), lambda i: (0, 0, 0))
    tail = pl.BlockSpec((1, rows, size), lambda i: (0, 0, points // size - 1))
    msgs = call(
        functools.partial(strip_kernel, n),
        [shape(rows + LABELS, iface + cap)] * n,
        grid=(1,),
        in_specs=[lead, tail, strip, tail] + [pl.BlockSpec(x.shape, lambda i, d=x.ndim: (0,) * d) for x in (stiff, face, face, weight)],
        out_specs=[pl.BlockSpec((rows + LABELS, iface + cap), lambda i: (0, 0))] * n,
    )(field, field, previous, previous, stiff, owner.reshape(1, iface), face, weight)

    got = [msgs[0]] + [None] * (n - 1)
    for k in range(n - 1, 0, -1):
        got[k] = lax.ppermute(msgs[k], "mer", [(i, i ^ k) for i in range(n)])

    tables = [table] + [lax.ppermute(table, "sub", [(i, i ^ k) for i in range(n_sub)]) for k in range(1, n_sub)]
    other = lax.ppermute(table, "grp", [(0, 1), (1, 0)])
    prod, double = call(
        functools.partial(synth_kernel, n_sub),
        [shape(chans, 3 * rows, dtype=BF16)] * 2,
        cost=(2 * 6 * rows * chans * chans, 4 * chans * chans),
        scratch_shapes=[pltpu.VMEM((chans, chans), F32)],
    )(*tables, other)

    part = 16
    band = pl.BlockSpec((1, part, points), lambda i: (0, i, 0))
    latest, prior = call(
        bulk_kernel,
        [shape(1, rows, points)] * 2,
        cost=(2 * 2 * 3 * rows * points * size, 16 * rows * points),
        grid=(rows // part,),
        in_specs=[band, band, pl.BlockSpec(stiff.shape, lambda i: (0, 0, 0))],
        out_specs=[band, band],
    )(field, previous, stiff)

    if n > 8:
        got = [jnp.stack(got)]
    summed, edges, ext = call(
        functools.partial(gather_kernel, n, iface, rows),
        [shape(n, rows, iface), shape(8, 128), shape(16, rows)],
        scratch_shapes=[pltpu.VMEM((n, 2 * rows, iface), BF16)],
    )(*got)
    crossed = lax.ppermute(summed, "grp", [(0, 1), (1, 0)])
    deep = -(-(n + 1) // 8) * 8
    compact = call(
        functools.partial(compact_kernel, n, iface, rows),
        shape(rows, iface),
        scratch_shapes=[pltpu.VMEM((deep, rows), F32), pltpu.VMEM((deep, rows), F32), pltpu.VMEM((deep, iface), F32)],
    )(*got)
    wide = max(2 * iface, -(-chans // 128) * 128)
    shares = call(
        functools.partial(share_kernel, n, n_sub, iface, rows),
        [shape(rows + LABELS, wide)] * n_sub,
    )(*got, summed, crossed, ext, compact, prod, double, table)
    parts = [
        lax.ppermute(shares[k], ("grp", "sub"), [(i, i ^ (n_sub + k)) for i in range(2 * n_sub)])
        for k in range(n_sub - 1, -1, -1)
    ]

    span = 2 * iface
    ends = pl.BlockSpec((1, rows, span), lambda i: (0, 0, i * (points // span - 1)))
    return tuple(
        call(
            functools.partial(patch_kernel, n_sub, iface, rows),
            [shape(1, rows, points)] * 2,
            grid=(2,),
            in_specs=[pl.BlockSpec((rows + LABELS, wide), lambda i: (0, 0))] * n_sub
            + [pl.BlockSpec((8, 128), lambda i: (0, 0)), pl.BlockSpec(stiff.shape, lambda i: (0, 0, 0)), ends, ends],
            out_specs=[ends, ends],
            scratch_shapes=[pltpu.VMEM((chans, LABELS), F32)],
            input_output_aliases={n_sub + 2: 0, n_sub + 3: 1},
        )(*parts, edges, stiff, latest, prior)
    )


def solution(mesh):
    in_specs = (
        P("grp", "sub", "mer"),
        P("grp", "sub", "mer"),
        P("grp", None, None),
        P("grp", None, "sub"),
        P("grp", "mer", None),
        P("grp", "mer"),
        P("grp", "mer"),
    )
    out_specs = (P("grp", "sub", "mer"), P("grp", "sub", "mer"))
    return jax.shard_map(body, mesh=mesh, in_specs=in_specs, out_specs=out_specs, check_vma=False)
```

```python
import functools

import jax
import jax.numpy as jnp
from jax import lax
from jax.experimental import pallas as pl
from jax.experimental.pallas import tpu as pltpu
from jax.sharding import PartitionSpec as P

F32 = jnp.float32
BF16 = jnp.bfloat16
HIGHEST = lax.Precision.HIGHEST
VMEM_BYTES = 48 * 2**20
LANES = 128
NT = (((1,), (1,)), ((), ()))


def split(x):
    high = x.astype(BF16)
    return high, (x - high.astype(F32)).astype(BF16)


def dot(a, b):
    return jnp.dot(a, b, preferred_element_type=F32)


def dot_nt(a, b):
    return lax.dot_general(a, b, NT, preferred_element_type=F32)


def times_matrix(x, matrix):
    rows, size = x.shape[0], matrix.shape[0]
    count = x.shape[1] // size
    tall = x if count == 1 else jnp.concatenate([x[:, e * size : (e + 1) * size] for e in range(count)], axis=0)
    high, low = split(tall)
    mh, ml = split(matrix)
    out = dot(high, mh) + (dot(low, mh) + dot(high, ml))
    if count == 1:
        return out
    return jnp.concatenate([out[e * rows : (e + 1) * rows] for e in range(count)], axis=1)


def neighbours(x):
    width = x.shape[1]
    col = lax.broadcasted_iota(jnp.int32, x.shape, 1)
    lower = jnp.where(col == 0, 0.0, pltpu.roll(x, 1, 1))
    higher = jnp.where(col == width - 1, 0.0, pltpu.roll(x, width - 1, 1))
    return lower + higher


def update(x, matrix):
    return 1.5 * x - 0.5 * times_matrix(x, matrix) + 0.25 * neighbours(x)


def layout(rows, iface, cap):
    cols, caps = iface // LANES, cap // LANES
    start = rows * (cols + caps)
    used = 2 * cols + caps + 2
    return cols, caps, start, start + -(-used // 8) * 8


def blocks(ref, start, rows, count):
    return jnp.concatenate([ref[start + j * rows : start + (j + 1) * rows, :] for j in range(count)], axis=1)


def strip_kernel(n, cap, field, previous, stiff, owner, face, weight, table, *refs):
    outs, copied = refs[:n], refs[n]
    wide_ref, fend_ref, prev_ref, pend_ref, stiff_ref, owner_ref, face_ref, weight_ref, sems = refs[n + 1 :]
    rows, iface = prev_ref.shape
    size = fend_ref.shape[1]
    points = field.shape[2]
    pairs = [
        (field.at[0, :, pl.ds(0, iface + size)], wide_ref),
        (previous.at[0, :, pl.ds(0, iface)], prev_ref),
        (stiff.at[0], stiff_ref),
        (field.at[0, :, pl.ds(points - size, size)], fend_ref),
        (previous.at[0, :, pl.ds(points - size, size)], pend_ref),
        (owner, owner_ref),
        (face, face_ref),
        (weight, weight_ref),
        (table, copied),
    ]
    copies = [pltpu.make_async_copy(a, b, sems.at[i]) for i, (a, b) in enumerate(pairs)]
    for copy in copies:
        copy.start()
    for copy in copies:
        copy.wait()
    me = lax.axis_index("mer")
    cols, caps, start, _ = layout(rows, iface, cap)
    matrix = stiff_ref[...]
    wide = wide_ref[...]
    strip = wide[:, :iface]
    nxt = (1.5 * strip - prev_ref[...] - 0.5 * times_matrix(strip, matrix)) + 0.25 * neighbours(wide)[:, :iface]
    fend = fend_ref[...]
    nend = update(fend, matrix) - pend_ref[...]
    owners = owner_ref[...]
    weights = weight_ref[...]
    faces = face_ref[...].astype(F32)
    target = owners.astype(F32) * float(iface) + faces
    count = -(-n // 8) * 8
    dest = lax.broadcasted_iota(jnp.int32, (count, iface), 0) ^ me
    match = jnp.where(owners == dest, 1.0, 0.0)
    before = lax.broadcasted_iota(jnp.int32, (iface, iface), 0) < lax.broadcasted_iota(jnp.int32, (iface, iface), 1)
    rank = dot(match.astype(BF16), jnp.where(before, 1.0, 0.0).astype(BF16))
    slots = jnp.where(match > 0.5, rank, -1.0)
    nh, nl = split(nxt * weights)
    fh, fl = split(jnp.concatenate([faces + 1.0, jnp.zeros((15, iface), F32)], axis=0))
    lhs = jnp.concatenate([nh, nl, fh, fl], axis=0)
    place = lax.broadcasted_iota(jnp.int32, (cap, iface), 0).astype(F32)
    lasts = jnp.transpose(jnp.concatenate([fend, nend], axis=0))[size - 1 : size, :]
    firsts = jnp.transpose(jnp.concatenate([nxt[:, :size], strip[:, :size]], axis=0))[0:1, :]
    for k in range(n):
        out = outs[k]
        chosen = jnp.where(slots[k : k + 1, :] == place, 1.0, 0.0).astype(BF16)
        got = dot_nt(lhs, chosen)
        picked = got[0:rows] + got[rows : 2 * rows]
        marks = got[2 * rows : 2 * rows + 1] + got[2 * rows + 16 : 2 * rows + 17] - 1.0
        for j in range(cols):
            span = slice(j * LANES, (j + 1) * LANES)
            out[j * rows : (j + 1) * rows, :] = strip[:, span]
            out[start + j : start + j + 1, :] = target[:, span]
            out[start + cols + j : start + cols + j + 1, :] = weights[:, span]
        for j in range(caps):
            span = slice(j * LANES, (j + 1) * LANES)
            out[(cols + j) * rows : (cols + j + 1) * rows, :] = picked[:, span]
            out[start + 2 * cols + j : start + 2 * cols + j + 1, :] = marks[:, span]
        out[start + 2 * cols + caps : start + 2 * cols + caps + 1, :] = lasts
        out[start + 2 * cols + caps + 1 : start + 2 * cols + caps + 2, :] = firsts


def bulk_kernel(field_ref, prev_ref, stiff_ref, latest_ref, prior_ref, llead_ref, plead_ref, ltail_ref, ptail_ref):
    matrix = stiff_ref[0]
    state = field_ref[0]
    first = update(state, matrix) - prev_ref[0]
    second = update(first, matrix) - state
    for value, whole, lead, tail in ((first, prior_ref, plead_ref, ptail_ref), (second, latest_ref, llead_ref, ltail_ref)):
        whole[0] = value
        lead[...] = value[:, : lead.shape[1]]
        tail[...] = value[:, value.shape[1] - tail.shape[1] :]


def synth_kernel(n_sub, *refs):
    own, other, full, prod_ref, double_ref = refs[0], refs[n_sub], refs[-1], refs[-3], refs[-2]
    sub = lax.axis_index("sub")
    rows = own.shape[0]
    for k in range(n_sub):
        start = pl.multiple_of((sub ^ k) * rows, rows)
        full[pl.ds(start, rows), :] = refs[k][...]

    def packed(x):
        high = x.astype(BF16).astype(F32)
        low = x - high
        return jnp.transpose(jnp.concatenate([high, low, high], axis=0)).astype(BF16)

    prod_ref[...] = packed(own[...])
    twice = 0.5 * jnp.dot(other[...], full[...], precision=HIGHEST, preferred_element_type=F32)
    double_ref[...] = packed(twice)


def message(refs, k):
    return refs[k] if len(refs) > 1 else refs[0].at[k]


def loop(n, body, init):
    if n <= 8:
        for k in range(n):
            init = body(k, init)
        return init
    return lax.fori_loop(0, n, body, init)


def hits(target, base, iface):
    return jnp.where(target - base == lax.broadcasted_iota(jnp.int32, (iface, iface), 0).astype(F32), 1.0, 0.0).astype(BF16)


def domain_base(me, k, iface):
    return ((me ^ k) * iface).astype(F32)


def labels(ref, rows, iface, cap):
    cols, _, start, _ = layout(rows, iface, cap)
    row = lambda first: jnp.concatenate([ref[first + j : first + j + 1, :] for j in range(cols)], axis=1)
    return row(start), row(start + cols)


def edge_rows(ref, rows, iface, cap):
    cols, caps, start, _ = layout(rows, iface, cap)
    at = start + 2 * cols + caps
    return ref[at : at + 1, :], ref[at + 1 : at + 2, :]


def gather_kernel(n, iface, cap, rows, *refs):
    msgs, (all_ref, edge_ref, ext_ref) = refs[:-6], refs[-4:-1]
    store = refs[-1]
    me = lax.axis_index("mer")
    edge_ref[...] = jnp.zeros(edge_ref.shape, F32)
    beyond = ((me + 1) * iface).astype(F32)

    def one(k, ext):
        ref = message(msgs, k)
        target, weight = labels(ref, rows, iface, cap)
        both = jnp.concatenate(split(blocks(ref, 0, rows, iface // LANES) * weight), axis=0)
        store[k] = both
        mask = jnp.broadcast_to(jnp.where(target == beyond, 1.0, 0.0), (16, iface)).astype(BF16)
        ext = ext + dot_nt(mask, both[:rows]) + dot_nt(mask, both[rows:])
        last, first = edge_rows(ref, rows, iface, cap)
        edge_ref[0:1, :] += jnp.where((me ^ k) == me - 1, 1.0, 0.0) * last
        edge_ref[1:2, :] += jnp.where((me ^ k) == me + 1, 1.0, 0.0) * first
        return ext

    ext_ref[...] = loop(n, one, jnp.zeros((16, rows), F32))
    last, first = edge_rows(message(msgs, 0), rows, iface, cap)
    lane = lax.broadcasted_iota(jnp.int32, last.shape, 1)
    edge_ref[0:1, :] += jnp.where(lane >= rows, jnp.where(me > 0, 0.25, 0.0) * first, 0.0)
    edge_ref[1:2, :] += jnp.where(lane < rows, jnp.where(me < n - 1, 0.25, 0.0) * last, 0.0)

    def onto(j, carry):
        base = domain_base(me, j, iface)

        def add(k, total):
            return total + dot_nt(store[k], hits(labels(message(msgs, k), rows, iface, cap)[0], base, iface))

        total = loop(n, add, jnp.zeros((2 * rows, iface), F32))
        all_ref[j] = total[:rows] + total[rows:]
        return carry

    loop(n, onto, 0)


def compact_kernel(n, iface, cap, rows, *refs):
    msgs, (out_ref,) = refs[:-4], refs[-4:-3]
    lasts, values, marks = refs[-3:]
    me = lax.axis_index("mer")
    cols, caps, start, _ = layout(rows, iface, cap)
    base = (me * iface).astype(F32)
    lasts[...] = jnp.zeros(lasts.shape, F32)
    values[...] = jnp.zeros(values.shape, F32)
    marks[...] = jnp.zeros(marks.shape, F32)
    face = lax.broadcasted_iota(jnp.int32, (iface, LANES), 0).astype(F32)
    line = lax.broadcasted_iota(jnp.int32, (1, iface), 1).astype(F32)

    def keep(k, carry):
        lasts[pl.ds((me ^ k) + 1, 1), :] = edge_rows(message(msgs, k), rows, iface, cap)[0]
        return carry

    loop(n, keep, 0)

    def one(k, total):
        ref = message(msgs, k)
        for j in range(caps):
            both = jnp.concatenate(split(ref[(cols + j) * rows : (cols + j + 1) * rows, :]), axis=0)
            marked = ref[start + 2 * cols + j : start + 2 * cols + j + 1, :]
            total = total + dot_nt(both, jnp.where(marked == face, 1.0, 0.0).astype(BF16))
        values[pl.ds(k, 1), :] = lasts[pl.ds(me ^ k, 1), :]
        target = ref[start : start + 1, 0:1] - base
        weight = 0.25 * ref[start + cols : start + cols + 1, 0:1]
        marks[pl.ds(k, 1), :] = jnp.where(target == line, weight, 0.0)
        return total

    total = loop(n, one, jnp.zeros((2 * rows, iface), F32))
    first = jnp.dot(jnp.transpose(values[...]), marks[...], precision=HIGHEST, preferred_element_type=F32)
    out_ref[...] = total[:rows] + total[rows:] + first[:rows]


def share_kernel(n, n_sub, iface, cap, rows, *refs):
    outs = refs[-n_sub:]
    zown_ref, zother_ref, ext_ref, compact_ref, prod_ref, double_ref, synth_ref = refs[-n_sub - 7 : -n_sub]
    msgs = refs[: -n_sub - 7]
    me = lax.axis_index("mer")
    sub = lax.axis_index("sub")
    base = (me * iface).astype(F32)
    cols = iface // LANES

    def add(k, total):
        target, weight = labels(message(msgs, k), rows, iface, cap)
        both = jnp.concatenate(split(zother_ref[k] * weight), axis=0)
        return total + dot_nt(both, hits(target, base, iface))

    total = loop(n, add, jnp.zeros((2 * rows, iface), F32))

    def tall(x):
        high, low = split(x)
        return jnp.concatenate([high, high, low], axis=0)

    y0, y1, y2 = tall(zown_ref[0]), tall(compact_ref[...]), tall(total[:rows] + total[rows:])
    ext = jnp.dot(ext_ref[0:8], synth_ref[...], precision=HIGHEST, preferred_element_type=F32)
    for k in range(n_sub):
        start = pl.multiple_of((sub ^ k) * rows, rows)
        prod = prod_ref[pl.ds(start, rows), :]
        force = (dot(prod, y0), dot(prod, y1) + dot(double_ref[pl.ds(start, rows), :], y2))
        for j in range(2 * cols):
            at = (j % cols) * LANES
            outs[k][j * rows : (j + 1) * rows, :] = force[j // cols][:, at : at + LANES]
        for j in range(ext.shape[1] // LANES):
            at = 2 * cols * rows + j
            outs[k][at : at + 1, :] = ext[0:1, j * LANES : (j + 1) * LANES]


def patch_kernel(n_sub, iface, rows, *refs):
    parts = refs[:n_sub]
    edge_ref, stiff_ref, llead, plead, ltail, ptail, _, _, latest_ref, prior_ref = refs[n_sub : n_sub + 10]
    lbuf, pbuf, lend, pend, turned, sems = refs[n_sub + 10 :]
    sub = lax.axis_index("sub")
    matrix = stiff_ref[0]
    size = matrix.shape[0]
    points = latest_ref.shape[2]
    cols = iface // LANES
    edges = jnp.transpose(edge_ref[...])

    def push(i, buf, out, start):
        copy = pltpu.make_async_copy(buf, out.at[0, :, pl.ds(start, buf.shape[1])], sems.at[i])
        copy.start()
        return copy

    total = functools.reduce(lambda a, b: a + b, [p[...] for p in parts])
    pick = lambda first: jnp.concatenate([total[(first + j) * rows : (first + j + 1) * rows] for j in range(cols)], axis=1)
    force, force1 = pick(0), pick(cols)
    col = lax.broadcasted_iota(jnp.int32, (rows, iface), 1)
    delta = 0.5 * force + jnp.where(col == 0, 0.25 * edges[0:rows, 0:1], 0.0)
    pbuf[...] = plead[...] + delta
    copies = [push(0, pbuf, prior_ref, 0)]
    ext = jnp.transpose(total[2 * cols * rows :])
    for j in range(turned.shape[0] // LANES):
        turned[j * LANES : (j + 1) * LANES, :] = ext[:, j : j + 1]
    beyond = edges[0:rows, 1:2] + 0.5 * turned[pl.ds(pl.multiple_of(sub * rows, rows), rows), :]
    end = lax.broadcasted_iota(jnp.int32, (rows, size), 1)
    shift = jnp.where(end == size - 1, 0.25 * edges[rows : 2 * rows, 1:2], 0.0)
    pend[...] = ptail[...] + shift
    copies.append(push(1, pend, prior_ref, points - size))
    lend[...] = ltail[...] + update(shift, matrix) + jnp.where(end == size - 1, 0.25 * beyond, 0.0)
    copies.append(push(2, lend, latest_ref, points - size))
    change = update(delta, matrix) + 0.5 * force1 + jnp.where(col == 0, 0.25 * edges[rows : 2 * rows, 0:1], 0.0)
    lbuf[:, 0:iface] = llead[:, 0:iface] + change
    lbuf[:, iface:] = llead[:, iface:] + jnp.where(end == 0, 0.25 * delta[:, iface - 1 : iface], 0.0)
    copies.append(push(3, lbuf, latest_ref, 0))
    for copy in copies:
        copy.wait()


def call(kernel, outs, cost=None, vmem=VMEM_BYTES, **more):
    params = pltpu.CompilerParams(vmem_limit_bytes=vmem)
    estimate = None if cost is None else pl.CostEstimate(flops=cost[0], bytes_accessed=cost[1], transcendentals=0)
    return pl.pallas_call(kernel, out_shape=outs, compiler_params=params, cost_estimate=estimate, **more)


def shape(*dims, dtype=F32):
    return jax.ShapeDtypeStruct(dims, dtype)


def body(field, previous, stiff, synth, owner, face, weight):
    n, n_sub = lax.axis_size("mer"), lax.axis_size("sub")
    _, rows, points = field.shape
    size = stiff.shape[1]
    iface = face.shape[1]
    chans = synth.shape[1]
    cap = -(-(2 * iface // n) // LANES) * LANES
    depth = layout(rows, iface, cap)[3]
    hbm = pl.BlockSpec(memory_space=pltpu.HBM)
    anywhere = pl.BlockSpec(memory_space=pl.ANY)
    vmem = pl.BlockSpec(memory_space=pltpu.VMEM)

    *msgs, table = call(
        functools.partial(strip_kernel, n, cap),
        [shape(depth, LANES)] * n + [shape(rows, chans)],
        vmem=None,
        in_specs=[hbm] * 7,
        out_specs=[vmem] * (n + 1),
        scratch_shapes=[
            pltpu.VMEM((rows, iface + size), F32),
            pltpu.VMEM((rows, size), F32),
            pltpu.VMEM((rows, iface), F32),
            pltpu.VMEM((rows, size), F32),
            pltpu.VMEM((size, size), F32),
            pltpu.VMEM((1, iface), jnp.int32),
            pltpu.VMEM((1, iface), jnp.int32),
            pltpu.VMEM((1, iface), F32),
            pltpu.SemaphoreType.DMA((9,)),
        ],
    )(field, previous, stiff, owner.reshape(1, iface), face, weight, jnp.transpose(synth[0]))

    got = [msgs[0]] + [None] * (n - 1)
    for k in range(n - 1, 0, -1):
        got[k] = lax.ppermute(msgs[k], "mer", [(i, i ^ k) for i in range(n)])

    tables = [table] + [lax.ppermute(table, "sub", [(i, i ^ k) for i in range(n_sub)]) for k in range(1, n_sub)]
    other = lax.ppermute(table, "grp", [(0, 1), (1, 0)])
    prod, double = call(
        functools.partial(synth_kernel, n_sub),
        [shape(chans, 3 * rows, dtype=BF16)] * 2,
        cost=(2 * 6 * rows * chans * chans, 4 * chans * chans),
        scratch_shapes=[pltpu.VMEM((chans, chans), F32)],
    )(*tables, other)

    part = 16
    band = pl.BlockSpec((1, part, points), lambda i: (0, i, 0))
    wide = [iface + size, iface, size, size]
    latest, prior, *ends = call(
        bulk_kernel,
        [shape(1, rows, points)] * 2 + [shape(rows, w) for w in wide],
        cost=(2 * 2 * 3 * rows * points * size, 16 * rows * points),
        grid=(rows // part,),
        in_specs=[band, band, pl.BlockSpec(stiff.shape, lambda i: (0, 0, 0))],
        out_specs=[band, band] + [pl.BlockSpec((part, w), lambda i: (i, 0)) for w in wide],
    )(field, previous, stiff)

    if n > 8:
        got = [jnp.stack(got)]
    summed, edges, ext = call(
        functools.partial(gather_kernel, n, iface, cap, rows),
        [shape(n, rows, iface), shape(8, 2 * rows), shape(16, rows)],
        in_specs=[vmem] * len(got) + [anywhere] * 2,
        scratch_shapes=[pltpu.VMEM((n, 2 * rows, iface), BF16)],
    )(*got, prod, double)
    crossed = lax.ppermute(summed, "grp", [(0, 1), (1, 0)])
    deep = -(-(n + 1) // 8) * 8
    compact = call(
        functools.partial(compact_kernel, n, iface, cap, rows),
        shape(rows, iface),
        scratch_shapes=[pltpu.VMEM((deep, LANES), F32), pltpu.VMEM((deep, LANES), F32), pltpu.VMEM((deep, iface), F32)],
    )(*got)
    tall = 2 * rows * (iface // LANES) + 8
    shares = call(
        functools.partial(share_kernel, n, n_sub, iface, cap, rows),
        [shape(tall, LANES)] * n_sub,
    )(*got, summed, crossed, ext, compact, prod, double, table)
    parts = [
        lax.ppermute(shares[k], ("grp", "sub"), [(i, i ^ (n_sub + k)) for i in range(2 * n_sub)])
        for k in range(n_sub - 1, -1, -1)
    ]

    return tuple(
        call(
            functools.partial(patch_kernel, n_sub, iface, rows),
            [shape(1, rows, points)] * 2,
            in_specs=[vmem] * (n_sub + 6) + [hbm] * 2,
            out_specs=[hbm] * 2,
            scratch_shapes=[
                pltpu.VMEM((rows, iface + size), F32),
                pltpu.VMEM((rows, iface), F32),
                pltpu.VMEM((rows, size), F32),
                pltpu.VMEM((rows, size), F32),
                pltpu.VMEM((chans, 1), F32),
                pltpu.SemaphoreType.DMA((4,)),
            ],
            input_output_aliases={n_sub + 6: 0, n_sub + 7: 1},
        )(*parts, edges, stiff, *ends, latest, prior)
    )


def solution(mesh):
    in_specs = (
        P("grp", "sub", "mer"),
        P("grp", "sub", "mer"),
        P("grp", None, None),
        P("grp", None, "sub"),
        P("grp", "mer", None),
        P("grp", "mer"),
        P("grp", "mer"),
    )
    out_specs = (P("grp", "sub", "mer"), P("grp", "sub", "mer"))
    return jax.shard_map(body, mesh=mesh, in_specs=in_specs, out_specs=out_specs, check_vma=False)
```

```python
import functools

import jax
import jax.numpy as jnp
from jax import lax
from jax.experimental import pallas as pl
from jax.experimental.pallas import tpu as pltpu
from jax.sharding import PartitionSpec as P

F32 = jnp.float32
BF16 = jnp.bfloat16
HIGHEST = lax.Precision.HIGHEST
VMEM_BYTES = 48 * 2**20
LANES = 128
NT = (((1,), (1,)), ((), ()))


def split(x):
    high = x.astype(BF16)
    return high, (x - high.astype(F32)).astype(BF16)


def dot(a, b):
    return jnp.dot(a, b, preferred_element_type=F32)


def dot_nt(a, b):
    return lax.dot_general(a, b, NT, preferred_element_type=F32)


def times_matrix(x, matrix):
    rows, size = x.shape[0], matrix.shape[0]
    count = x.shape[1] // size
    tall = x if count == 1 else jnp.concatenate([x[:, e * size : (e + 1) * size] for e in range(count)], axis=0)
    high, low = split(tall)
    mh, ml = split(matrix)
    out = dot(high, mh) + (dot(low, mh) + dot(high, ml))
    if count == 1:
        return out
    return jnp.concatenate([out[e * rows : (e + 1) * rows] for e in range(count)], axis=1)


def neighbours(x):
    width = x.shape[1]
    col = lax.broadcasted_iota(jnp.int32, x.shape, 1)
    lower = jnp.where(col == 0, 0.0, pltpu.roll(x, 1, 1))
    higher = jnp.where(col == width - 1, 0.0, pltpu.roll(x, width - 1, 1))
    return lower + higher


def update(x, matrix):
    return 1.5 * x - 0.5 * times_matrix(x, matrix) + 0.25 * neighbours(x)


def layout(rows, iface, cap):
    cols, caps = iface // LANES, cap // LANES
    start = rows * (cols + caps)
    used = 2 * cols + caps + 2
    return cols, caps, start, start + -(-used // 8) * 8


def blocks(ref, start, rows, count):
    return jnp.concatenate([ref[start + j * rows : start + (j + 1) * rows, :] for j in range(count)], axis=1)


def strip_kernel(n, cap, field, previous, stiff, owner, face, weight, table, *refs):
    outs, copied = refs[:n], refs[n]
    wide_ref, fend_ref, prev_ref, pend_ref, stiff_ref, owner_ref, face_ref, weight_ref, sems = refs[n + 1 :]
    rows, iface = prev_ref.shape
    size = fend_ref.shape[1]
    points = field.shape[2]
    pairs = [
        (field.at[0, :, pl.ds(0, iface + size)], wide_ref),
        (previous.at[0, :, pl.ds(0, iface)], prev_ref),
        (stiff.at[0], stiff_ref),
        (field.at[0, :, pl.ds(points - size, size)], fend_ref),
        (previous.at[0, :, pl.ds(points - size, size)], pend_ref),
        (owner, owner_ref),
        (face, face_ref),
        (weight, weight_ref),
        (table, copied),
    ]
    copies = [pltpu.make_async_copy(a, b, sems.at[i]) for i, (a, b) in enumerate(pairs)]
    for copy in copies:
        copy.start()
    for copy in copies:
        copy.wait()
    me = lax.axis_index("mer")
    cols, caps, start, _ = layout(rows, iface, cap)
    matrix = stiff_ref[...]
    wide = wide_ref[...]
    strip = wide[:, :iface]
    nxt = (1.5 * strip - prev_ref[...] - 0.5 * times_matrix(strip, matrix)) + 0.25 * neighbours(wide)[:, :iface]
    fend = fend_ref[...]
    nend = update(fend, matrix) - pend_ref[...]
    owners = owner_ref[...]
    weights = weight_ref[...]
    faces = face_ref[...].astype(F32)
    target = owners.astype(F32) * float(iface) + faces
    count = -(-n // 8) * 8
    dest = lax.broadcasted_iota(jnp.int32, (count, iface), 0) ^ me
    match = jnp.where(owners == dest, 1.0, 0.0)
    before = lax.broadcasted_iota(jnp.int32, (iface, iface), 0) < lax.broadcasted_iota(jnp.int32, (iface, iface), 1)
    rank = dot(match.astype(BF16), jnp.where(before, 1.0, 0.0).astype(BF16))
    slots = jnp.where(match > 0.5, rank, -1.0)
    nh, nl = split(nxt * weights)
    fh, fl = split(jnp.concatenate([faces + 1.0, jnp.zeros((15, iface), F32)], axis=0))
    lhs = jnp.concatenate([nh, nl, fh, fl], axis=0)
    place = lax.broadcasted_iota(jnp.int32, (cap, iface), 0).astype(F32)
    lasts = jnp.transpose(jnp.concatenate([fend, nend], axis=0))[size - 1 : size, :]
    firsts = jnp.transpose(jnp.concatenate([nxt[:, :size], strip[:, :size]], axis=0))[0:1, :]
    for k in range(n):
        out = outs[k]
        chosen = jnp.where(slots[k : k + 1, :] == place, 1.0, 0.0).astype(BF16)
        got = dot_nt(lhs, chosen)
        picked = got[0:rows] + got[rows : 2 * rows]
        marks = got[2 * rows : 2 * rows + 1] + got[2 * rows + 16 : 2 * rows + 17] - 1.0
        for j in range(cols):
            span = slice(j * LANES, (j + 1) * LANES)
            out[j * rows : (j + 1) * rows, :] = strip[:, span]
            out[start + j : start + j + 1, :] = target[:, span]
            out[start + cols + j : start + cols + j + 1, :] = weights[:, span]
        for j in range(caps):
            span = slice(j * LANES, (j + 1) * LANES)
            out[(cols + j) * rows : (cols + j + 1) * rows, :] = picked[:, span]
            out[start + 2 * cols + j : start + 2 * cols + j + 1, :] = marks[:, span]
        out[start + 2 * cols + caps : start + 2 * cols + caps + 1, :] = lasts
        out[start + 2 * cols + caps + 1 : start + 2 * cols + caps + 2, :] = firsts


def bulk_kernel(field_ref, prev_ref, stiff_ref, latest_ref, prior_ref, llead_ref, plead_ref, ltail_ref, ptail_ref):
    matrix = stiff_ref[0]
    state = field_ref[0]
    first = update(state, matrix) - prev_ref[0]
    second = update(first, matrix) - state
    for value, whole, lead, tail in ((first, prior_ref, plead_ref, ptail_ref), (second, latest_ref, llead_ref, ltail_ref)):
        whole[0] = value
        lead[...] = value[:, : lead.shape[1]]
        tail[...] = value[:, value.shape[1] - tail.shape[1] :]


def packed(x):
    high = x.astype(BF16).astype(F32)
    low = x - high
    return jnp.transpose(jnp.concatenate([high, low, high], axis=0)).astype(BF16)


def tall(x):
    high, low = split(x)
    return jnp.concatenate([high, high, low], axis=0)


def synth_kernel(table_ref, prod_ref):
    prod_ref[...] = packed(table_ref[...])


def arrival(n):
    return [0, *range(2, n), 1] if n > 1 else [0]


def message(refs, k):
    return refs[arrival(len(refs)).index(k)] if len(refs) > 1 else refs[0].at[k]


def loop(n, body, init):
    if n <= 8:
        for k in range(n):
            init = body(k, init)
        return init
    return lax.fori_loop(0, n, body, init)


def hits(target, base, iface):
    return jnp.where(target - base == lax.broadcasted_iota(jnp.int32, (iface, iface), 0).astype(F32), 1.0, 0.0).astype(BF16)


def domain_base(me, k, iface):
    return ((me ^ k) * iface).astype(F32)


def labels(ref, rows, iface, cap):
    cols, _, start, _ = layout(rows, iface, cap)
    row = lambda first: jnp.concatenate([ref[first + j : first + j + 1, :] for j in range(cols)], axis=1)
    return row(start), row(start + cols)


def edge_rows(ref, rows, iface, cap):
    cols, caps, start, _ = layout(rows, iface, cap)
    at = start + 2 * cols + caps
    return ref[at : at + 1, :], ref[at + 1 : at + 2, :]


def gather_kernel(n, iface, cap, rows, count, *refs):
    msgs, table_ref, (all_ref, edge_ref, ext_ref) = refs[:count], refs[-5], refs[-4:-1]
    store = refs[-1]
    me = lax.axis_index("mer")
    edge_ref[...] = jnp.zeros(edge_ref.shape, F32)
    beyond = ((me + 1) * iface).astype(F32)

    def one(k, ext):
        ref = message(msgs, k)
        target, weight = labels(ref, rows, iface, cap)
        both = jnp.concatenate(split(blocks(ref, 0, rows, iface // LANES) * weight), axis=0)
        store[k] = both
        mask = jnp.broadcast_to(jnp.where(target == beyond, 1.0, 0.0), (16, iface)).astype(BF16)
        ext = ext + dot_nt(mask, both[:rows]) + dot_nt(mask, both[rows:])
        last, first = edge_rows(ref, rows, iface, cap)
        edge_ref[0:1, :] += jnp.where((me ^ k) == me - 1, 1.0, 0.0) * last
        edge_ref[1:2, :] += jnp.where((me ^ k) == me + 1, 1.0, 0.0) * first
        return ext

    ext_ref[...] = loop(n, one, jnp.zeros((16, rows), F32))
    last, first = edge_rows(message(msgs, 0), rows, iface, cap)
    lane = lax.broadcasted_iota(jnp.int32, last.shape, 1)
    edge_ref[0:1, :] += jnp.where(lane >= rows, jnp.where(me > 0, 0.25, 0.0) * first, 0.0)
    edge_ref[1:2, :] += jnp.where(lane < rows, jnp.where(me < n - 1, 0.25, 0.0) * last, 0.0)

    def onto(j, carry):
        base = domain_base(me, j, iface)

        def add(k, total):
            return total + dot_nt(store[k], hits(labels(message(msgs, k), rows, iface, cap)[0], base, iface))

        total = loop(n, add, jnp.zeros((2 * rows, iface), F32))
        all_ref[pl.ds(j * rows, rows), 0:iface] = total[:rows] + total[rows:]
        return carry

    loop(n, onto, 0)
    all_ref[n * rows :, 0 : table_ref.shape[1]] = table_ref[...]


def compact_kernel(n, n_sub, iface, cap, rows, *refs):
    msgs, (zown_ref, prod_ref), tables = refs[: -n_sub - 8], refs[-n_sub - 8 : -n_sub - 6], refs[-n_sub - 6 : -6]
    force_ref, high_ref, low_ref = refs[-6:-3]
    lasts, values, marks = refs[-3:]
    me = lax.axis_index("mer")
    cols, caps, start, _ = layout(rows, iface, cap)
    base = (me * iface).astype(F32)
    lasts[...] = jnp.zeros(lasts.shape, F32)
    values[...] = jnp.zeros(values.shape, F32)
    marks[...] = jnp.zeros(marks.shape, F32)
    face = lax.broadcasted_iota(jnp.int32, (iface, LANES), 0).astype(F32)
    line = lax.broadcasted_iota(jnp.int32, (1, iface), 1).astype(F32)

    def keep(k, carry):
        lasts[pl.ds((me ^ k) + 1, 1), :] = edge_rows(message(msgs, k), rows, iface, cap)[0]
        return carry

    loop(n, keep, 0)

    def one(k, total):
        ref = message(msgs, k)
        for j in range(caps):
            both = jnp.concatenate(split(ref[(cols + j) * rows : (cols + j + 1) * rows, :]), axis=0)
            marked = ref[start + 2 * cols + j : start + 2 * cols + j + 1, :]
            total = total + dot_nt(both, jnp.where(marked == face, 1.0, 0.0).astype(BF16))
        values[pl.ds(k, 1), :] = lasts[pl.ds(me ^ k, 1), :]
        target = ref[start : start + 1, 0:1] - base
        weight = 0.25 * ref[start + cols : start + cols + 1, 0:1]
        marks[pl.ds(k, 1), :] = jnp.where(target == line, weight, 0.0)
        return total

    total = loop(n, one, jnp.zeros((2 * rows, iface), F32))
    first = jnp.dot(jnp.transpose(values[...]), marks[...], precision=HIGHEST, preferred_element_type=F32)
    prod = prod_ref[...]
    force_ref[:, 0:iface] = dot(prod, tall(zown_ref[0:rows, 0:iface]))
    force_ref[:, iface:] = dot(prod, tall(total[:rows] + total[rows:] + first[:rows]))
    for k in range(n_sub):
        start = pl.multiple_of((lax.axis_index("sub") ^ k) * rows, rows)
        high_ref[pl.ds(start, rows), :], low_ref[pl.ds(start, rows), :] = split(tables[k][...])


def share_kernel(n, n_sub, iface, cap, rows, *refs):
    outs, more_ref = refs[-n_sub - 1 : -1], refs[-1]
    zother_ref, ext_ref, force_ref, high_ref, low_ref, synth_ref = refs[-n_sub - 7 : -n_sub - 1]
    msgs = refs[: -n_sub - 7]
    me = lax.axis_index("mer")
    sub = lax.axis_index("sub")
    base = (me * iface).astype(F32)
    cols = iface // LANES
    chans = synth_ref.shape[1]
    high, low = split(0.5 * zother_ref[n * rows :, 0:chans])
    double = packed(dot(high, high_ref[...]) + (dot(low, high_ref[...]) + dot(high, low_ref[...])))

    def add(k, total):
        target, weight = labels(message(msgs, k), rows, iface, cap)
        both = jnp.concatenate(split(zother_ref[pl.ds(k * rows, rows), 0:iface] * weight), axis=0)
        return total + dot_nt(both, hits(target, base, iface))

    total = loop(n, add, jnp.zeros((2 * rows, iface), F32))
    more = dot(double, tall(total[:rows] + total[rows:]))
    ext = jnp.dot(ext_ref[0:8], synth_ref[...], precision=HIGHEST, preferred_element_type=F32)
    more_ref[...] = more
    for k in range(n_sub):
        start = pl.multiple_of((sub ^ k) * rows, rows)
        for j in range(2 * cols):
            span = slice(j * LANES, (j + 1) * LANES)
            value = force_ref[pl.ds(start, rows), span]
            if j >= cols:
                value = value + more_ref[pl.ds(start, rows), (j - cols) * LANES : (j - cols + 1) * LANES]
            outs[k][j * rows : (j + 1) * rows, :] = value
        for j in range(chans // LANES):
            at = 2 * cols * rows + j
            outs[k][at : at + 1, :] = ext[0:1, j * LANES : (j + 1) * LANES]


def patch_kernel(n_sub, iface, rows, *refs):
    parts = refs[:n_sub]
    edge_ref, stiff_ref, llead, plead, ltail, ptail, _, _, latest_ref, prior_ref = refs[n_sub : n_sub + 10]
    lbuf, pbuf, lend, pend, turned, sems = refs[n_sub + 10 :]
    sub = lax.axis_index("sub")
    matrix = stiff_ref[0]
    size = matrix.shape[0]
    points = latest_ref.shape[2]
    cols = iface // LANES
    edges = jnp.transpose(edge_ref[...])

    def push(i, buf, out, start):
        copy = pltpu.make_async_copy(buf, out.at[0, :, pl.ds(start, buf.shape[1])], sems.at[i])
        copy.start()
        return copy

    total = functools.reduce(lambda a, b: a + b, [p[...] for p in parts])
    pick = lambda first: jnp.concatenate([total[(first + j) * rows : (first + j + 1) * rows] for j in range(cols)], axis=1)
    force, force1 = pick(0), pick(cols)
    col = lax.broadcasted_iota(jnp.int32, (rows, iface), 1)
    delta = 0.5 * force + jnp.where(col == 0, 0.25 * edges[0:rows, 0:1], 0.0)
    pbuf[...] = plead[...] + delta
    copies = [push(0, pbuf, prior_ref, 0)]
    ext = jnp.transpose(total[2 * cols * rows :])
    for j in range(turned.shape[0] // LANES):
        turned[j * LANES : (j + 1) * LANES, :] = ext[:, j : j + 1]
    beyond = edges[0:rows, 1:2] + 0.5 * turned[pl.ds(pl.multiple_of(sub * rows, rows), rows), :]
    end = lax.broadcasted_iota(jnp.int32, (rows, size), 1)
    shift = jnp.where(end == size - 1, 0.25 * edges[rows : 2 * rows, 1:2], 0.0)
    pend[...] = ptail[...] + shift
    copies.append(push(1, pend, prior_ref, points - size))
    lend[...] = ltail[...] + update(shift, matrix) + jnp.where(end == size - 1, 0.25 * beyond, 0.0)
    copies.append(push(2, lend, latest_ref, points - size))
    change = update(delta, matrix) + 0.5 * force1 + jnp.where(col == 0, 0.25 * edges[rows : 2 * rows, 0:1], 0.0)
    lbuf[:, 0:iface] = llead[:, 0:iface] + change
    lbuf[:, iface:] = llead[:, iface:] + jnp.where(end == 0, 0.25 * delta[:, iface - 1 : iface], 0.0)
    copies.append(push(3, lbuf, latest_ref, 0))
    for copy in copies:
        copy.wait()


def call(kernel, outs, cost=None, vmem=VMEM_BYTES, **more):
    params = pltpu.CompilerParams(vmem_limit_bytes=vmem)
    estimate = None if cost is None else pl.CostEstimate(flops=cost[0], bytes_accessed=cost[1], transcendentals=0)
    return pl.pallas_call(kernel, out_shape=outs, compiler_params=params, cost_estimate=estimate, **more)


def shape(*dims, dtype=F32):
    return jax.ShapeDtypeStruct(dims, dtype)


def body(field, previous, stiff, synth, owner, face, weight):
    n, n_sub = lax.axis_size("mer"), lax.axis_size("sub")
    _, rows, points = field.shape
    size = stiff.shape[1]
    iface = face.shape[1]
    chans = synth.shape[1]
    cap = -(-(2 * iface // n) // LANES) * LANES
    depth = layout(rows, iface, cap)[3]
    hbm = pl.BlockSpec(memory_space=pltpu.HBM)
    anywhere = pl.BlockSpec(memory_space=pl.ANY)
    vmem = pl.BlockSpec(memory_space=pltpu.VMEM)

    *msgs, table = call(
        functools.partial(strip_kernel, n, cap),
        [shape(depth, LANES)] * n + [shape(rows, chans)],
        in_specs=[hbm] * 7,
        out_specs=[vmem] * (n + 1),
        scratch_shapes=[
            pltpu.VMEM((rows, iface + size), F32),
            pltpu.VMEM((rows, size), F32),
            pltpu.VMEM((rows, iface), F32),
            pltpu.VMEM((rows, size), F32),
            pltpu.VMEM((size, size), F32),
            pltpu.VMEM((1, iface), jnp.int32),
            pltpu.VMEM((1, iface), jnp.int32),
            pltpu.VMEM((1, iface), F32),
            pltpu.SemaphoreType.DMA((9,)),
        ],
    )(*[pltpu.with_memory_space_constraint(v, pltpu.HBM) for v in (field, previous, stiff, owner.reshape(1, iface), face, weight, jnp.transpose(synth[0]))])

    got = [msgs[0]] + [lax.ppermute(msgs[k], "mer", [(i, i ^ k) for i in range(n)]) for k in arrival(n)[1:]]

    tables = [table] + [lax.ppermute(table, "sub", [(i, i ^ k) for i in range(n_sub)]) for k in range(1, n_sub)]
    prod = call(synth_kernel, shape(chans, 3 * rows, dtype=BF16))(table)

    part = 16
    band = pl.BlockSpec((1, part, points), lambda i: (0, i, 0))
    wide = [iface + size, iface, size, size]
    latest, prior, *ends = call(
        bulk_kernel,
        [shape(1, rows, points)] * 2 + [shape(rows, w) for w in wide],
        cost=(2 * 2 * 3 * rows * points * size, 16 * rows * points),
        grid=(rows // part,),
        in_specs=[band, band, pl.BlockSpec(stiff.shape, lambda i: (0, 0, 0))],
        out_specs=[band, band] + [pl.BlockSpec((part, w), lambda i: (i, 0)) for w in wide],
    )(field, previous, stiff)

    if n > 8:
        got = [jnp.stack([got[arrival(n).index(k)] for k in range(n)])]
    summed, edges, ext = call(
        functools.partial(gather_kernel, n, iface, cap, rows, len(got)),
        [shape((n + 1) * rows, max(iface, chans)), shape(8, 2 * rows), shape(16, rows)],
        in_specs=[vmem] * len(got) + [anywhere] * n_sub + [vmem],
        scratch_shapes=[pltpu.VMEM((n, 2 * rows, iface), BF16)],
    )(*got, prod, *tables[1:], table)
    crossed = lax.ppermute(summed, "grp", [(0, 1), (1, 0)])
    deep = -(-(n + 1) // 8) * 8
    forces, high, low = call(
        functools.partial(compact_kernel, n, n_sub, iface, cap, rows),
        [shape(chans, 2 * iface), shape(chans, chans, dtype=BF16), shape(chans, chans, dtype=BF16)],
        scratch_shapes=[pltpu.VMEM((deep, LANES), F32), pltpu.VMEM((deep, LANES), F32), pltpu.VMEM((deep, iface), F32)],
    )(*got, summed, prod, *tables)
    height = 2 * rows * (iface // LANES) + 8
    shares = call(
        functools.partial(share_kernel, n, n_sub, iface, cap, rows),
        [shape(height, LANES)] * n_sub,
        scratch_shapes=[pltpu.VMEM((chans, iface), F32)],
    )(*got, crossed, ext, forces, high, low, table)
    parts = [
        lax.ppermute(shares[k], ("grp", "sub"), [(i, i ^ (n_sub + k)) for i in range(2 * n_sub)])
        for k in [*range(1, n_sub), 0]
    ]

    return tuple(
        call(
            functools.partial(patch_kernel, n_sub, iface, rows),
            [shape(1, rows, points)] * 2,
            in_specs=[vmem] * (n_sub + 6) + [hbm] * 2,
            out_specs=[hbm] * 2,
            scratch_shapes=[
                pltpu.VMEM((rows, iface + size), F32),
                pltpu.VMEM((rows, iface), F32),
                pltpu.VMEM((rows, size), F32),
                pltpu.VMEM((rows, size), F32),
                pltpu.VMEM((chans, 1), F32),
                pltpu.SemaphoreType.DMA((4,)),
            ],
            input_output_aliases={n_sub + 6: 0, n_sub + 7: 1},
        )(*parts, edges, stiff, *ends, latest, prior)
    )


def solution(mesh):
    in_specs = (
        P("grp", "sub", "mer"),
        P("grp", "sub", "mer"),
        P("grp", None, None),
        P("grp", None, "sub"),
        P("grp", "mer", None),
        P("grp", "mer"),
        P("grp", "mer"),
    )
    out_specs = (P("grp", "sub", "mer"), P("grp", "sub", "mer"))
    return jax.shard_map(body, mesh=mesh, in_specs=in_specs, out_specs=out_specs, check_vma=False)
```

```python
import functools

import jax
import jax.numpy as jnp
from jax import lax
from jax.experimental import pallas as pl
from jax.experimental.pallas import tpu as pltpu
from jax.sharding import PartitionSpec as P

F32 = jnp.float32
BF16 = jnp.bfloat16
HIGHEST = lax.Precision.HIGHEST
VMEM_BYTES = 48 * 2**20
LANES = 128
NT = (((1,), (1,)), ((), ()))


def split(x):
    high = x.astype(BF16)
    return high, (x - high.astype(F32)).astype(BF16)


def dot(a, b):
    return jnp.dot(a, b, preferred_element_type=F32)


def dot_nt(a, b):
    return lax.dot_general(a, b, NT, preferred_element_type=F32)


def times_matrix(x, matrix):
    rows, size = x.shape[0], matrix.shape[0]
    count = x.shape[1] // size
    tall = x if count == 1 else jnp.concatenate([x[:, e * size : (e + 1) * size] for e in range(count)], axis=0)
    high, low = split(tall)
    mh, ml = split(matrix)
    out = dot(high, mh) + (dot(low, mh) + dot(high, ml))
    if count == 1:
        return out
    return jnp.concatenate([out[e * rows : (e + 1) * rows] for e in range(count)], axis=1)


def neighbours(x):
    width = x.shape[1]
    col = lax.broadcasted_iota(jnp.int32, x.shape, 1)
    lower = jnp.where(col == 0, 0.0, pltpu.roll(x, 1, 1))
    higher = jnp.where(col == width - 1, 0.0, pltpu.roll(x, width - 1, 1))
    return lower + higher


def update(x, matrix):
    return 1.5 * x - 0.5 * times_matrix(x, matrix) + 0.25 * neighbours(x)


def layout(rows, iface, cap):
    cols, caps = iface // LANES, cap // LANES
    start = rows * (cols + caps)
    used = 2 * cols + caps + 2
    return cols, caps, start, start + -(-used // 8) * 8


def blocks(ref, start, rows, count):
    return jnp.concatenate([ref[start + j * rows : start + (j + 1) * rows, :] for j in range(count)], axis=1)


def strip_kernel(n, cap, field, previous, stiff, owner, face, weight, table, *refs):
    outs, copied = refs[:n], refs[n]
    wide_ref, fend_ref, prev_ref, pend_ref, stiff_ref, owner_ref, face_ref, weight_ref, chosen_ref, sems = refs[n + 1 :]
    rows, iface = prev_ref.shape
    size = fend_ref.shape[1]
    points = field.shape[2]
    pairs = [
        (owner, owner_ref),
        (face, face_ref),
        (weight, weight_ref),
        (stiff.at[0], stiff_ref),
        (field.at[0, :, pl.ds(0, iface + size)], wide_ref),
        (previous.at[0, :, pl.ds(0, iface)], prev_ref),
        (field.at[0, :, pl.ds(points - size, size)], fend_ref),
        (previous.at[0, :, pl.ds(points - size, size)], pend_ref),
        (table, copied),
    ]
    copies = [pltpu.make_async_copy(a, b, sems.at[i]) for i, (a, b) in enumerate(pairs)]
    for copy in copies:
        copy.start()
    me = lax.axis_index("mer")
    cols, caps, start, _ = layout(rows, iface, cap)
    count = -(-n // 8) * 8
    dest = lax.broadcasted_iota(jnp.int32, (count, iface), 0) ^ me
    before = lax.broadcasted_iota(jnp.int32, (iface, iface), 0) < lax.broadcasted_iota(jnp.int32, (iface, iface), 1)
    place = lax.broadcasted_iota(jnp.int32, (cap, iface), 0).astype(F32)
    for copy in copies[:3]:
        copy.wait()
    owners = owner_ref[...]
    weights = weight_ref[...]
    faces = face_ref[...].astype(F32)
    target = owners.astype(F32) * float(iface) + faces
    match = jnp.where(owners == dest, 1.0, 0.0)
    rank = dot(match.astype(BF16), jnp.where(before, 1.0, 0.0).astype(BF16))
    slots = jnp.where(match > 0.5, rank, -1.0)
    for k in range(n):
        chosen_ref[k] = jnp.where(slots[k : k + 1, :] == place, 1.0, 0.0).astype(BF16)
    for copy in copies[3:]:
        copy.wait()
    matrix = stiff_ref[...]
    wide = wide_ref[...]
    strip = wide[:, :iface]
    nxt = (1.5 * strip - prev_ref[...] - 0.5 * times_matrix(strip, matrix)) + 0.25 * neighbours(wide)[:, :iface]
    fend = fend_ref[...]
    nend = update(fend, matrix) - pend_ref[...]
    nh, nl = split(nxt * weights)
    fh, fl = split(jnp.concatenate([faces + 1.0, jnp.zeros((15, iface), F32)], axis=0))
    lhs = jnp.concatenate([nh, nl, fh, fl], axis=0)
    lasts = jnp.transpose(jnp.concatenate([fend, nend], axis=0))[size - 1 : size, :]
    firsts = jnp.transpose(jnp.concatenate([nxt[:, :size], strip[:, :size]], axis=0))[0:1, :]
    for k in range(n):
        out = outs[k]
        got = dot_nt(lhs, chosen_ref[k])
        picked = got[0:rows] + got[rows : 2 * rows]
        marks = got[2 * rows : 2 * rows + 1] + got[2 * rows + 16 : 2 * rows + 17] - 1.0
        for j in range(cols):
            span = slice(j * LANES, (j + 1) * LANES)
            out[j * rows : (j + 1) * rows, :] = strip[:, span]
            out[start + j : start + j + 1, :] = target[:, span]
            out[start + cols + j : start + cols + j + 1, :] = weights[:, span]
        for j in range(caps):
            span = slice(j * LANES, (j + 1) * LANES)
            out[(cols + j) * rows : (cols + j + 1) * rows, :] = picked[:, span]
            out[start + 2 * cols + j : start + 2 * cols + j + 1, :] = marks[:, span]
        out[start + 2 * cols + caps : start + 2 * cols + caps + 1, :] = lasts
        out[start + 2 * cols + caps + 1 : start + 2 * cols + caps + 2, :] = firsts


def bulk_kernel(field_ref, prev_ref, stiff_ref, latest_ref, prior_ref, llead_ref, plead_ref, ltail_ref, ptail_ref):
    matrix = stiff_ref[0]
    state = field_ref[0]
    first = update(state, matrix) - prev_ref[0]
    second = update(first, matrix) - state
    for value, whole, lead, tail in ((first, prior_ref, plead_ref, ptail_ref), (second, latest_ref, llead_ref, ltail_ref)):
        whole[0] = value
        lead[...] = value[:, : lead.shape[1]]
        tail[...] = value[:, value.shape[1] - tail.shape[1] :]


def packed(x):
    high = x.astype(BF16).astype(F32)
    low = x - high
    return jnp.transpose(jnp.concatenate([high, low, high], axis=0)).astype(BF16)


def tall(x):
    high, low = split(x)
    return jnp.concatenate([high, high, low], axis=0)


def synth_kernel(table_ref, prod_ref):
    prod_ref[...] = packed(table_ref[...])


def arrival(n):
    return [0, *range(2, n), 1] if n > 1 else [0]


def message(refs, k):
    return refs[arrival(len(refs)).index(k)] if len(refs) > 1 else refs[0].at[k]


def loop(n, body, init):
    if n <= 8:
        for k in range(n):
            init = body(k, init)
        return init
    return lax.fori_loop(0, n, body, init)


def hits(target, base, iface):
    return jnp.where(target - base == lax.broadcasted_iota(jnp.int32, (iface, iface), 0).astype(F32), 1.0, 0.0).astype(BF16)


def domain_base(me, k, iface):
    return ((me ^ k) * iface).astype(F32)


def labels(ref, rows, iface, cap):
    cols, _, start, _ = layout(rows, iface, cap)
    row = lambda first: jnp.concatenate([ref[first + j : first + j + 1, :] for j in range(cols)], axis=1)
    return row(start), row(start + cols)


def edge_rows(ref, rows, iface, cap):
    cols, caps, start, _ = layout(rows, iface, cap)
    at = start + 2 * cols + caps
    return ref[at : at + 1, :], ref[at + 1 : at + 2, :]


def gather_kernel(n, iface, cap, rows, count, *refs):
    msgs, table_ref, (all_ref, edge_ref, ext_ref) = refs[:count], refs[-5], refs[-4:-1]
    store = refs[-1]
    me = lax.axis_index("mer")
    edge_ref[...] = jnp.zeros(edge_ref.shape, F32)
    beyond = ((me + 1) * iface).astype(F32)

    def one(k, ext):
        ref = message(msgs, k)
        target, weight = labels(ref, rows, iface, cap)
        both = jnp.concatenate(split(blocks(ref, 0, rows, iface // LANES) * weight), axis=0)
        store[k] = both
        mask = jnp.broadcast_to(jnp.where(target == beyond, 1.0, 0.0), (16, iface)).astype(BF16)
        ext = ext + dot_nt(mask, both[:rows]) + dot_nt(mask, both[rows:])
        last, first = edge_rows(ref, rows, iface, cap)
        edge_ref[0:1, :] += jnp.where((me ^ k) == me - 1, 1.0, 0.0) * last
        edge_ref[1:2, :] += jnp.where((me ^ k) == me + 1, 1.0, 0.0) * first
        return ext

    ext_ref[...] = loop(n, one, jnp.zeros((16, rows), F32))
    last, first = edge_rows(message(msgs, 0), rows, iface, cap)
    lane = lax.broadcasted_iota(jnp.int32, last.shape, 1)
    edge_ref[0:1, :] += jnp.where(lane >= rows, jnp.where(me > 0, 0.25, 0.0) * first, 0.0)
    edge_ref[1:2, :] += jnp.where(lane < rows, jnp.where(me < n - 1, 0.25, 0.0) * last, 0.0)

    def onto(j, carry):
        base = domain_base(me, j, iface)

        def add(k, total):
            return total + dot_nt(store[k], hits(labels(message(msgs, k), rows, iface, cap)[0], base, iface))

        total = loop(n, add, jnp.zeros((2 * rows, iface), F32))
        all_ref[pl.ds(j * rows, rows), 0:iface] = total[:rows] + total[rows:]
        return carry

    loop(n, onto, 0)
    all_ref[n * rows :, 0 : table_ref.shape[1]] = table_ref[...]


def compact_kernel(n, n_sub, iface, cap, rows, count, *refs):
    msgs, (zown_ref, ext_ref, prod_ref), tables = refs[:count], refs[count : count + 3], refs[count + 3 : count + 3 + n_sub]
    high_ref, low_ref, hit_ref, *outs = refs[count + 3 + n_sub : -4]
    force_ref = refs[-4]
    sub = lax.axis_index("sub")
    lasts, values, marks = refs[-3:]
    me = lax.axis_index("mer")
    cols, caps, start, _ = layout(rows, iface, cap)
    base = (me * iface).astype(F32)
    lasts[...] = jnp.zeros(lasts.shape, F32)
    values[...] = jnp.zeros(values.shape, F32)
    marks[...] = jnp.zeros(marks.shape, F32)
    face = lax.broadcasted_iota(jnp.int32, (iface, LANES), 0).astype(F32)
    line = lax.broadcasted_iota(jnp.int32, (1, iface), 1).astype(F32)

    def keep(k, carry):
        lasts[pl.ds((me ^ k) + 1, 1), :] = edge_rows(message(msgs, k), rows, iface, cap)[0]
        return carry

    loop(n, keep, 0)

    def one(k, total):
        ref = message(msgs, k)
        for j in range(caps):
            both = jnp.concatenate(split(ref[(cols + j) * rows : (cols + j + 1) * rows, :]), axis=0)
            marked = ref[start + 2 * cols + j : start + 2 * cols + j + 1, :]
            total = total + dot_nt(both, jnp.where(marked == face, 1.0, 0.0).astype(BF16))
        values[pl.ds(k, 1), :] = lasts[pl.ds(me ^ k, 1), :]
        target = ref[start : start + 1, 0:1] - base
        weight = 0.25 * ref[start + cols : start + cols + 1, 0:1]
        marks[pl.ds(k, 1), :] = jnp.where(target == line, weight, 0.0)
        hit_ref[k] = hits(labels(ref, rows, iface, cap)[0], base, iface)
        return total

    total = loop(n, one, jnp.zeros((2 * rows, iface), F32))
    first = jnp.dot(jnp.transpose(values[...]), marks[...], precision=HIGHEST, preferred_element_type=F32)
    prod = prod_ref[...]
    force_ref[:, 0:iface] = dot(prod, tall(zown_ref[0:rows, 0:iface]))
    force_ref[:, iface:] = dot(prod, tall(total[:rows] + total[rows:] + first[:rows]))
    ext = jnp.dot(ext_ref[0:8], tables[0][...], precision=HIGHEST, preferred_element_type=F32)
    for k in range(n_sub):
        where = pl.ds(pl.multiple_of((sub ^ k) * rows, rows), rows)
        high_ref[where, :], low_ref[where, :] = split(tables[k][...])
        for j in range(2 * cols):
            outs[k][j * rows : (j + 1) * rows, :] = force_ref[where, j * LANES : (j + 1) * LANES]
        for j in range(ext.shape[1] // LANES):
            at = 2 * cols * rows + j
            outs[k][at : at + 1, :] = ext[0:1, j * LANES : (j + 1) * LANES]


def share_kernel(n, n_sub, iface, cap, rows, *refs):
    msgs, (zother_ref, high_ref, low_ref, hit_ref) = refs[: -2 * n_sub - 5], refs[-2 * n_sub - 5 : -2 * n_sub - 1]
    begun, outs, more_ref = refs[-2 * n_sub - 1 : -n_sub - 1], refs[-n_sub - 1 : -1], refs[-1]
    sub = lax.axis_index("sub")
    cols = iface // LANES
    high, low = split(0.5 * zother_ref[n * rows :, 0 : high_ref.shape[1]])
    double = packed(dot(high, high_ref[...]) + (dot(low, high_ref[...]) + dot(high, low_ref[...])))

    def add(k, total):
        weight = labels(message(msgs, k), rows, iface, cap)[1]
        both = jnp.concatenate(split(zother_ref[pl.ds(k * rows, rows), 0:iface] * weight), axis=0)
        return total + dot_nt(both, hit_ref[k])

    total = loop(n, add, jnp.zeros((2 * rows, iface), F32))
    more_ref[...] = dot(double, tall(total[:rows] + total[rows:]))
    for k in range(n_sub):
        where = pl.ds(pl.multiple_of((sub ^ k) * rows, rows), rows)
        outs[k][: cols * rows, :] = begun[k][: cols * rows, :]
        outs[k][2 * cols * rows :, :] = begun[k][2 * cols * rows :, :]
        for j in range(cols):
            span = slice((cols + j) * rows, (cols + j + 1) * rows)
            outs[k][span, :] = begun[k][span, :] + more_ref[where, j * LANES : (j + 1) * LANES]


def patch_kernel(n_sub, iface, rows, *refs):
    parts = refs[:n_sub]
    edge_ref, stiff_ref, llead, plead, ltail, ptail, _, _, latest_ref, prior_ref = refs[n_sub : n_sub + 10]
    lbuf, pbuf, lend, pend, turned, sems = refs[n_sub + 10 :]
    sub = lax.axis_index("sub")
    matrix = stiff_ref[0]
    size = matrix.shape[0]
    points = latest_ref.shape[2]
    cols = iface // LANES
    edges = jnp.transpose(edge_ref[...])

    def push(i, buf, out, start):
        copy = pltpu.make_async_copy(buf, out.at[0, :, pl.ds(start, buf.shape[1])], sems.at[i])
        copy.start()
        return copy

    total = functools.reduce(lambda a, b: a + b, [p[...] for p in parts])
    pick = lambda first: jnp.concatenate([total[(first + j) * rows : (first + j + 1) * rows] for j in range(cols)], axis=1)
    force, force1 = pick(0), pick(cols)
    col = lax.broadcasted_iota(jnp.int32, (rows, iface), 1)
    delta = 0.5 * force + jnp.where(col == 0, 0.25 * edges[0:rows, 0:1], 0.0)
    pbuf[...] = plead[...] + delta
    copies = [push(0, pbuf, prior_ref, 0)]
    end = lax.broadcasted_iota(jnp.int32, (rows, size), 1)
    change = update(delta, matrix) + 0.5 * force1 + jnp.where(col == 0, 0.25 * edges[rows : 2 * rows, 0:1], 0.0)
    lbuf[:, 0:iface] = llead[:, 0:iface] + change
    lbuf[:, iface:] = llead[:, iface:] + jnp.where(end == 0, 0.25 * delta[:, iface - 1 : iface], 0.0)
    copies.append(push(3, lbuf, latest_ref, 0))
    shift = jnp.where(end == size - 1, 0.25 * edges[rows : 2 * rows, 1:2], 0.0)
    pend[...] = ptail[...] + shift
    copies.append(push(1, pend, prior_ref, points - size))
    ext = jnp.transpose(total[2 * cols * rows :])
    for j in range(turned.shape[0] // LANES):
        turned[j * LANES : (j + 1) * LANES, :] = ext[:, j : j + 1]
    beyond = edges[0:rows, 1:2] + 0.5 * turned[pl.ds(pl.multiple_of(sub * rows, rows), rows), :]
    lend[...] = ltail[...] + update(shift, matrix) + jnp.where(end == size - 1, 0.25 * beyond, 0.0)
    copies.append(push(2, lend, latest_ref, points - size))
    for copy in copies:
        copy.wait()


def call(kernel, outs, cost=None, vmem=VMEM_BYTES, **more):
    params = pltpu.CompilerParams(vmem_limit_bytes=vmem)
    estimate = None if cost is None else pl.CostEstimate(flops=cost[0], bytes_accessed=cost[1], transcendentals=0)
    return pl.pallas_call(kernel, out_shape=outs, compiler_params=params, cost_estimate=estimate, **more)


def shape(*dims, dtype=F32):
    return jax.ShapeDtypeStruct(dims, dtype)


def body(field, previous, stiff, synth, owner, face, weight):
    n, n_sub = lax.axis_size("mer"), lax.axis_size("sub")
    _, rows, points = field.shape
    size = stiff.shape[1]
    iface = face.shape[1]
    chans = synth.shape[1]
    cap = -(-(2 * iface // n) // LANES) * LANES
    depth = layout(rows, iface, cap)[3]
    hbm = pl.BlockSpec(memory_space=pltpu.HBM)
    anywhere = pl.BlockSpec(memory_space=pl.ANY)
    vmem = pl.BlockSpec(memory_space=pltpu.VMEM)

    *msgs, table = call(
        functools.partial(strip_kernel, n, cap),
        [shape(depth, LANES)] * n + [shape(rows, chans)],
        in_specs=[hbm] * 7,
        out_specs=[vmem] * (n + 1),
        scratch_shapes=[
            pltpu.VMEM((rows, iface + size), F32),
            pltpu.VMEM((rows, size), F32),
            pltpu.VMEM((rows, iface), F32),
            pltpu.VMEM((rows, size), F32),
            pltpu.VMEM((size, size), F32),
            pltpu.VMEM((1, iface), jnp.int32),
            pltpu.VMEM((1, iface), jnp.int32),
            pltpu.VMEM((1, iface), F32),
            pltpu.VMEM((n, cap, iface), BF16),
            pltpu.SemaphoreType.DMA((9,)),
        ],
    )(*[pltpu.with_memory_space_constraint(v, pltpu.HBM) for v in (field, previous, stiff, owner.reshape(1, iface), face, weight, jnp.transpose(synth[0]))])

    got = [msgs[0]] + [lax.ppermute(msgs[k], "mer", [(i, i ^ k) for i in range(n)]) for k in arrival(n)[1:]]

    tables = [table] + [lax.ppermute(table, "sub", [(i, i ^ k) for i in range(n_sub)]) for k in range(1, n_sub)]
    prod = call(synth_kernel, shape(chans, 3 * rows, dtype=BF16))(table)

    part = 16
    band = pl.BlockSpec((1, part, points), lambda i: (0, i, 0))
    wide = [iface + size, iface, size, size]
    latest, prior, *ends = call(
        bulk_kernel,
        [shape(1, rows, points)] * 2 + [shape(rows, w) for w in wide],
        cost=(2 * 2 * 3 * rows * points * size, 16 * rows * points),
        grid=(rows // part,),
        in_specs=[band, band, pl.BlockSpec(stiff.shape, lambda i: (0, 0, 0))],
        out_specs=[band, band] + [pl.BlockSpec((part, w), lambda i: (i, 0)) for w in wide],
    )(field, previous, stiff)

    if n > 8:
        got = [jnp.stack([got[arrival(n).index(k)] for k in range(n)])]
    summed, edges, ext = call(
        functools.partial(gather_kernel, n, iface, cap, rows, len(got)),
        [shape((n + 1) * rows, max(iface, chans)), shape(8, 2 * rows), shape(16, rows)],
        in_specs=[vmem] * len(got) + [anywhere] * n_sub + [vmem],
        scratch_shapes=[pltpu.VMEM((n, 2 * rows, iface), BF16)],
    )(*got, prod, *tables[1:], table)
    crossed = lax.ppermute(summed, "grp", [(0, 1), (1, 0)])
    deep = -(-(n + 1) // 8) * 8
    height = 2 * rows * (iface // LANES) + 8
    part_shapes = [shape(height, LANES)] * n_sub
    high, low, hit, *begun = call(
        functools.partial(compact_kernel, n, n_sub, iface, cap, rows, len(got)),
        [shape(chans, chans, dtype=BF16)] * 2 + [shape(n, iface, iface, dtype=BF16)] + part_shapes,
        scratch_shapes=[
            pltpu.VMEM((chans, 2 * iface), F32),
            pltpu.VMEM((deep, LANES), F32),
            pltpu.VMEM((deep, LANES), F32),
            pltpu.VMEM((deep, iface), F32),
        ],
    )(*got, summed, ext, prod, *tables)
    shares = call(
        functools.partial(share_kernel, n, n_sub, iface, cap, rows),
        part_shapes,
        scratch_shapes=[pltpu.VMEM((chans, iface), F32)],
    )(*got, crossed, high, low, hit, *begun)
    parts = [
        lax.ppermute(shares[k], ("grp", "sub"), [(i, i ^ (n_sub + k)) for i in range(2 * n_sub)])
        for k in [*range(1, n_sub), 0]
    ]

    return tuple(
        call(
            functools.partial(patch_kernel, n_sub, iface, rows),
            [shape(1, rows, points)] * 2,
            in_specs=[vmem] * (n_sub + 6) + [hbm] * 2,
            out_specs=[hbm] * 2,
            scratch_shapes=[
                pltpu.VMEM((rows, iface + size), F32),
                pltpu.VMEM((rows, iface), F32),
                pltpu.VMEM((rows, size), F32),
                pltpu.VMEM((rows, size), F32),
                pltpu.VMEM((chans, 1), F32),
                pltpu.SemaphoreType.DMA((4,)),
            ],
            input_output_aliases={n_sub + 6: 0, n_sub + 7: 1},
        )(*parts, edges, stiff, *ends, latest, prior)
    )


def solution(mesh):
    in_specs = (
        P("grp", "sub", "mer"),
        P("grp", "sub", "mer"),
        P("grp", None, None),
        P("grp", None, "sub"),
        P("grp", "mer", None),
        P("grp", "mer"),
        P("grp", "mer"),
    )
    out_specs = (P("grp", "sub", "mer"), P("grp", "sub", "mer"))
    return jax.shard_map(body, mesh=mesh, in_specs=in_specs, out_specs=out_specs, check_vma=False)
```

```python
import functools

import jax
import jax.numpy as jnp
from jax import lax
from jax.experimental import pallas as pl
from jax.experimental.pallas import tpu as pltpu
from jax.sharding import PartitionSpec as P

F32 = jnp.float32
BF16 = jnp.bfloat16
HIGHEST = lax.Precision.HIGHEST
VMEM_BYTES = 48 * 2**20
LANES = 128
LONG = (10**10, 10**6)
NT = (((1,), (1,)), ((), ()))


def split(x):
    high = x.astype(BF16)
    return high, (x - high.astype(F32)).astype(BF16)


def dot(a, b):
    return jnp.dot(a, b, preferred_element_type=F32)


def dot_nt(a, b):
    return lax.dot_general(a, b, NT, preferred_element_type=F32)


def times_matrix(x, matrix):
    rows, size = x.shape[0], matrix.shape[0]
    count = x.shape[1] // size
    tall = x if count == 1 else jnp.concatenate([x[:, e * size : (e + 1) * size] for e in range(count)], axis=0)
    high, low = split(tall)
    mh, ml = split(matrix)
    out = dot(high, mh) + (dot(low, mh) + dot(high, ml))
    if count == 1:
        return out
    return jnp.concatenate([out[e * rows : (e + 1) * rows] for e in range(count)], axis=1)


def neighbours(x):
    width = x.shape[1]
    col = lax.broadcasted_iota(jnp.int32, x.shape, 1)
    lower = jnp.where(col == 0, 0.0, pltpu.roll(x, 1, 1))
    higher = jnp.where(col == width - 1, 0.0, pltpu.roll(x, width - 1, 1))
    return lower + higher


def update(x, matrix):
    return 1.5 * x - 0.5 * times_matrix(x, matrix) + 0.25 * neighbours(x)


def layout(rows, iface, cap):
    cols, caps = iface // LANES, cap // LANES
    start = rows * (cols + caps)
    used = 2 * cols + caps + 2
    return cols, caps, start, start + -(-used // 8) * 8


def blocks(ref, start, rows, count):
    return jnp.concatenate([ref[start + j * rows : start + (j + 1) * rows, :] for j in range(count)], axis=1)


def strip_kernel(n, cap, field, previous, stiff, owner, face, weight, table, *refs):
    outs, copied = refs[:n], refs[n]
    wide_ref, fend_ref, prev_ref, pend_ref, stiff_ref, owner_ref, face_ref, weight_ref, chosen_ref, sems = refs[n + 1 :]
    rows, iface = prev_ref.shape
    size = fend_ref.shape[1]
    points = field.shape[2]
    pairs = [
        (owner, owner_ref),
        (face, face_ref),
        (weight, weight_ref),
        (stiff.at[0], stiff_ref),
        (field.at[0, :, pl.ds(0, iface + size)], wide_ref),
        (previous.at[0, :, pl.ds(0, iface)], prev_ref),
        (field.at[0, :, pl.ds(points - size, size)], fend_ref),
        (previous.at[0, :, pl.ds(points - size, size)], pend_ref),
        (table, copied),
    ]
    copies = [pltpu.make_async_copy(a, b, sems.at[i]) for i, (a, b) in enumerate(pairs)]
    for copy in copies:
        copy.start()
    me = lax.axis_index("mer")
    cols, caps, start, _ = layout(rows, iface, cap)
    count = -(-n // 8) * 8
    dest = lax.broadcasted_iota(jnp.int32, (count, iface), 0) ^ me
    before = lax.broadcasted_iota(jnp.int32, (iface, iface), 0) < lax.broadcasted_iota(jnp.int32, (iface, iface), 1)
    place = lax.broadcasted_iota(jnp.int32, (cap, iface), 0).astype(F32)
    for copy in copies[:3]:
        copy.wait()
    owners = owner_ref[...]
    weights = weight_ref[...]
    faces = face_ref[...].astype(F32)
    target = owners.astype(F32) * float(iface) + faces
    match = jnp.where(owners == dest, 1.0, 0.0)
    rank = dot(match.astype(BF16), jnp.where(before, 1.0, 0.0).astype(BF16))
    slots = jnp.where(match > 0.5, rank, -1.0)
    for k in range(n):
        chosen_ref[k] = jnp.where(slots[k : k + 1, :] == place, 1.0, 0.0).astype(BF16)
    for copy in copies[3:]:
        copy.wait()
    matrix = stiff_ref[...]
    wide = wide_ref[...]
    strip = wide[:, :iface]
    nxt = (1.5 * strip - prev_ref[...] - 0.5 * times_matrix(strip, matrix)) + 0.25 * neighbours(wide)[:, :iface]
    fend = fend_ref[...]
    nend = update(fend, matrix) - pend_ref[...]
    nh, nl = split(nxt * weights)
    fh, fl = split(jnp.concatenate([faces + 1.0, jnp.zeros((15, iface), F32)], axis=0))
    lhs = jnp.concatenate([nh, nl, fh, fl], axis=0)
    lasts = jnp.transpose(jnp.concatenate([fend, nend], axis=0))[size - 1 : size, :]
    firsts = jnp.transpose(jnp.concatenate([nxt[:, :size], strip[:, :size]], axis=0))[0:1, :]
    for k in range(n):
        out = outs[k]
        got = dot_nt(lhs, chosen_ref[k])
        picked = got[0:rows] + got[rows : 2 * rows]
        marks = got[2 * rows : 2 * rows + 1] + got[2 * rows + 16 : 2 * rows + 17] - 1.0
        for j in range(cols):
            span = slice(j * LANES, (j + 1) * LANES)
            out[j * rows : (j + 1) * rows, :] = strip[:, span]
            out[start + j : start + j + 1, :] = target[:, span]
            out[start + cols + j : start + cols + j + 1, :] = weights[:, span]
        for j in range(caps):
            span = slice(j * LANES, (j + 1) * LANES)
            out[(cols + j) * rows : (cols + j + 1) * rows, :] = picked[:, span]
            out[start + 2 * cols + j : start + 2 * cols + j + 1, :] = marks[:, span]
        out[start + 2 * cols + caps : start + 2 * cols + caps + 1, :] = lasts
        out[start + 2 * cols + caps + 1 : start + 2 * cols + caps + 2, :] = firsts


def bulk_kernel(field_ref, prev_ref, stiff_ref, latest_ref, prior_ref, llead_ref, plead_ref, ltail_ref, ptail_ref):
    matrix = stiff_ref[0]
    state = field_ref[0]
    first = update(state, matrix) - prev_ref[0]
    second = update(first, matrix) - state
    for value, whole, lead, tail in ((first, prior_ref, plead_ref, ptail_ref), (second, latest_ref, llead_ref, ltail_ref)):
        whole[0] = value
        lead[...] = value[:, : lead.shape[1]]
        tail[...] = value[:, value.shape[1] - tail.shape[1] :]


def packed(x):
    high = x.astype(BF16).astype(F32)
    low = x - high
    return jnp.transpose(jnp.concatenate([high, low, high], axis=0)).astype(BF16)


def tall(x):
    high, low = split(x)
    return jnp.concatenate([high, high, low], axis=0)


def synth_kernel(table_ref, prod_ref):
    prod_ref[...] = packed(table_ref[...])


def arrival(n):
    half = n // 2
    return [0, *([half] if half else []), *[k for k in range(1, n) if k != half]]


def message(refs, k):
    return refs[arrival(len(refs)).index(k)] if len(refs) > 1 else refs[0].at[k]


def loop(n, body, init):
    if n <= 8:
        for k in range(n):
            init = body(k, init)
        return init
    return lax.fori_loop(0, n, body, init)


def hits(target, base, iface):
    return jnp.where(target - base == lax.broadcasted_iota(jnp.int32, (iface, iface), 0).astype(F32), 1.0, 0.0).astype(BF16)


def domain_base(me, k, iface):
    return ((me ^ k) * iface).astype(F32)


def labels(ref, rows, iface, cap):
    cols, _, start, _ = layout(rows, iface, cap)
    row = lambda first: jnp.concatenate([ref[first + j : first + j + 1, :] for j in range(cols)], axis=1)
    return row(start), row(start + cols)


def edge_rows(ref, rows, iface, cap):
    cols, caps, start, _ = layout(rows, iface, cap)
    at = start + 2 * cols + caps
    return ref[at : at + 1, :], ref[at + 1 : at + 2, :]


def gather_kernel(n, iface, cap, rows, count, *refs):
    msgs, table_ref, (all_ref, edge_ref, ext_ref) = refs[:count], refs[-5], refs[-4:-1]
    store = refs[-1]
    me = lax.axis_index("mer")
    edge_ref[...] = jnp.zeros(edge_ref.shape, F32)
    beyond = ((me + 1) * iface).astype(F32)

    def one(k, ext):
        ref = message(msgs, k)
        target, weight = labels(ref, rows, iface, cap)
        both = jnp.concatenate(split(blocks(ref, 0, rows, iface // LANES) * weight), axis=0)
        store[k] = both
        mask = jnp.broadcast_to(jnp.where(target == beyond, 1.0, 0.0), (16, iface)).astype(BF16)
        ext = ext + dot_nt(mask, both[:rows]) + dot_nt(mask, both[rows:])
        last, first = edge_rows(ref, rows, iface, cap)
        edge_ref[0:1, :] += jnp.where((me ^ k) == me - 1, 1.0, 0.0) * last
        edge_ref[1:2, :] += jnp.where((me ^ k) == me + 1, 1.0, 0.0) * first
        return ext

    ext_ref[...] = loop(n, one, jnp.zeros((16, rows), F32))
    last, first = edge_rows(message(msgs, 0), rows, iface, cap)
    lane = lax.broadcasted_iota(jnp.int32, last.shape, 1)
    edge_ref[0:1, :] += jnp.where(lane >= rows, jnp.where(me > 0, 0.25, 0.0) * first, 0.0)
    edge_ref[1:2, :] += jnp.where(lane < rows, jnp.where(me < n - 1, 0.25, 0.0) * last, 0.0)

    def onto(j, carry):
        base = domain_base(me, j, iface)

        def add(k, total):
            return total + dot_nt(store[k], hits(labels(message(msgs, k), rows, iface, cap)[0], base, iface))

        total = loop(n, add, jnp.zeros((2 * rows, iface), F32))
        all_ref[pl.ds(j * rows, rows), 0:iface] = total[:rows] + total[rows:]
        return carry

    loop(n, onto, 0)
    all_ref[n * rows :, 0 : table_ref.shape[1]] = table_ref[...]


def compact_kernel(n, n_sub, iface, cap, rows, count, *refs):
    msgs, (zown_ref, ext_ref, prod_ref), tables = refs[:count], refs[count : count + 3], refs[count + 3 : count + 3 + n_sub]
    high_ref, low_ref, hit_ref, *outs = refs[count + 3 + n_sub : -4]
    force_ref = refs[-4]
    sub = lax.axis_index("sub")
    lasts, values, marks = refs[-3:]
    me = lax.axis_index("mer")
    cols, caps, start, _ = layout(rows, iface, cap)
    base = (me * iface).astype(F32)
    lasts[...] = jnp.zeros(lasts.shape, F32)
    values[...] = jnp.zeros(values.shape, F32)
    marks[...] = jnp.zeros(marks.shape, F32)
    face = lax.broadcasted_iota(jnp.int32, (iface, LANES), 0).astype(F32)
    line = lax.broadcasted_iota(jnp.int32, (1, iface), 1).astype(F32)

    def keep(k, carry):
        lasts[pl.ds((me ^ k) + 1, 1), :] = edge_rows(message(msgs, k), rows, iface, cap)[0]
        return carry

    loop(n, keep, 0)

    def one(k, total):
        ref = message(msgs, k)
        for j in range(caps):
            both = jnp.concatenate(split(ref[(cols + j) * rows : (cols + j + 1) * rows, :]), axis=0)
            marked = ref[start + 2 * cols + j : start + 2 * cols + j + 1, :]
            total = total + dot_nt(both, jnp.where(marked == face, 1.0, 0.0).astype(BF16))
        values[pl.ds(k, 1), :] = lasts[pl.ds(me ^ k, 1), :]
        target = ref[start : start + 1, 0:1] - base
        weight = 0.25 * ref[start + cols : start + cols + 1, 0:1]
        marks[pl.ds(k, 1), :] = jnp.where(target == line, weight, 0.0)
        hit_ref[k] = hits(labels(ref, rows, iface, cap)[0], base, iface)
        return total

    total = loop(n, one, jnp.zeros((2 * rows, iface), F32))
    first = jnp.dot(jnp.transpose(values[...]), marks[...], precision=HIGHEST, preferred_element_type=F32)
    prod = prod_ref[...]
    force_ref[:, 0:iface] = dot(prod, tall(zown_ref[0:rows, 0:iface]))
    force_ref[:, iface:] = dot(prod, tall(total[:rows] + total[rows:] + first[:rows]))
    ext = jnp.dot(ext_ref[0:8], tables[0][...], precision=HIGHEST, preferred_element_type=F32)
    for k in range(n_sub):
        where = pl.ds(pl.multiple_of((sub ^ k) * rows, rows), rows)
        high_ref[where, :], low_ref[where, :] = split(tables[k][...])
        for j in range(2 * cols):
            outs[k][j * rows : (j + 1) * rows, :] = force_ref[where, j * LANES : (j + 1) * LANES]
        for j in range(ext.shape[1] // LANES):
            at = 2 * cols * rows + j
            outs[k][at : at + 1, :] = ext[0:1, j * LANES : (j + 1) * LANES]


def share_kernel(n, n_sub, iface, cap, rows, *refs):
    msgs, (zother_ref, high_ref, low_ref, hit_ref) = refs[: -2 * n_sub - 5], refs[-2 * n_sub - 5 : -2 * n_sub - 1]
    begun, outs, more_ref = refs[-2 * n_sub - 1 : -n_sub - 1], refs[-n_sub - 1 : -1], refs[-1]
    sub = lax.axis_index("sub")
    cols = iface // LANES
    high, low = split(0.5 * zother_ref[n * rows :, 0 : high_ref.shape[1]])
    double = packed(dot(high, high_ref[...]) + (dot(low, high_ref[...]) + dot(high, low_ref[...])))

    def add(k, total):
        weight = labels(message(msgs, k), rows, iface, cap)[1]
        both = jnp.concatenate(split(zother_ref[pl.ds(k * rows, rows), 0:iface] * weight), axis=0)
        return total + dot_nt(both, hit_ref[k])

    total = loop(n, add, jnp.zeros((2 * rows, iface), F32))
    more_ref[...] = dot(double, tall(total[:rows] + total[rows:]))
    for k in range(n_sub):
        where = pl.ds(pl.multiple_of((sub ^ k) * rows, rows), rows)
        outs[k][: cols * rows, :] = begun[k][: cols * rows, :]
        outs[k][2 * cols * rows :, :] = begun[k][2 * cols * rows :, :]
        for j in range(cols):
            span = slice((cols + j) * rows, (cols + j + 1) * rows)
            outs[k][span, :] = begun[k][span, :] + more_ref[where, j * LANES : (j + 1) * LANES]


def patch_kernel(n_sub, iface, rows, *refs):
    parts = refs[:n_sub]
    edge_ref, stiff_ref, llead, plead, ltail, ptail, _, _, latest_ref, prior_ref = refs[n_sub : n_sub + 10]
    lbuf, pbuf, lend, pend, turned, sems = refs[n_sub + 10 :]
    sub = lax.axis_index("sub")
    matrix = stiff_ref[0]
    size = matrix.shape[0]
    points = latest_ref.shape[2]
    cols = iface // LANES
    edges = jnp.transpose(edge_ref[...])

    def push(i, buf, out, start):
        copy = pltpu.make_async_copy(buf, out.at[0, :, pl.ds(start, buf.shape[1])], sems.at[i])
        copy.start()
        return copy

    total = functools.reduce(lambda a, b: a + b, [p[...] for p in parts])
    pick = lambda first: jnp.concatenate([total[(first + j) * rows : (first + j + 1) * rows] for j in range(cols)], axis=1)
    force, force1 = pick(0), pick(cols)
    col = lax.broadcasted_iota(jnp.int32, (rows, iface), 1)
    delta = 0.5 * force + jnp.where(col == 0, 0.25 * edges[0:rows, 0:1], 0.0)
    pbuf[...] = plead[...] + delta
    copies = [push(0, pbuf, prior_ref, 0)]
    end = lax.broadcasted_iota(jnp.int32, (rows, size), 1)
    change = update(delta, matrix) + 0.5 * force1 + jnp.where(col == 0, 0.25 * edges[rows : 2 * rows, 0:1], 0.0)
    lbuf[:, 0:iface] = llead[:, 0:iface] + change
    lbuf[:, iface:] = llead[:, iface:] + jnp.where(end == 0, 0.25 * delta[:, iface - 1 : iface], 0.0)
    copies.append(push(3, lbuf, latest_ref, 0))
    shift = jnp.where(end == size - 1, 0.25 * edges[rows : 2 * rows, 1:2], 0.0)
    pend[...] = ptail[...] + shift
    copies.append(push(1, pend, prior_ref, points - size))
    ext = jnp.transpose(total[2 * cols * rows :])
    for j in range(turned.shape[0] // LANES):
        turned[j * LANES : (j + 1) * LANES, :] = ext[:, j : j + 1]
    beyond = edges[0:rows, 1:2] + 0.5 * turned[pl.ds(pl.multiple_of(sub * rows, rows), rows), :]
    lend[...] = ltail[...] + update(shift, matrix) + jnp.where(end == size - 1, 0.25 * beyond, 0.0)
    copies.append(push(2, lend, latest_ref, points - size))
    for copy in copies:
        copy.wait()


def call(kernel, outs, cost=None, vmem=VMEM_BYTES, **more):
    params = pltpu.CompilerParams(vmem_limit_bytes=vmem)
    estimate = None if cost is None else pl.CostEstimate(flops=cost[0], bytes_accessed=cost[1], transcendentals=0)
    return pl.pallas_call(kernel, out_shape=outs, compiler_params=params, cost_estimate=estimate, **more)


def shape(*dims, dtype=F32):
    return jax.ShapeDtypeStruct(dims, dtype)


def body(field, previous, stiff, synth, owner, face, weight):
    n, n_sub = lax.axis_size("mer"), lax.axis_size("sub")
    _, rows, points = field.shape
    size = stiff.shape[1]
    iface = face.shape[1]
    chans = synth.shape[1]
    cap = -(-(2 * iface // n) // LANES) * LANES
    depth = layout(rows, iface, cap)[3]
    hbm = pl.BlockSpec(memory_space=pltpu.HBM)
    anywhere = pl.BlockSpec(memory_space=pl.ANY)
    vmem = pl.BlockSpec(memory_space=pltpu.VMEM)

    *msgs, table = call(
        functools.partial(strip_kernel, n, cap),
        [shape(depth, LANES)] * n + [shape(rows, chans)],
        in_specs=[hbm] * 7,
        out_specs=[vmem] * (n + 1),
        scratch_shapes=[
            pltpu.VMEM((rows, iface + size), F32),
            pltpu.VMEM((rows, size), F32),
            pltpu.VMEM((rows, iface), F32),
            pltpu.VMEM((rows, size), F32),
            pltpu.VMEM((size, size), F32),
            pltpu.VMEM((1, iface), jnp.int32),
            pltpu.VMEM((1, iface), jnp.int32),
            pltpu.VMEM((1, iface), F32),
            pltpu.VMEM((n, cap, iface), BF16),
            pltpu.SemaphoreType.DMA((9,)),
        ],
    )(*[pltpu.with_memory_space_constraint(v, pltpu.HBM) for v in (field, previous, stiff, owner.reshape(1, iface), face, weight, jnp.transpose(synth[0]))])

    got = [msgs[0]] + [lax.ppermute(msgs[k], "mer", [(i, i ^ k) for i in range(n)]) for k in arrival(n)[1:]]

    tables = [table] + [lax.ppermute(table, "sub", [(i, i ^ k) for i in range(n_sub)]) for k in range(1, n_sub)]
    prod = call(synth_kernel, shape(chans, 3 * rows, dtype=BF16))(table)

    part = 16
    band = pl.BlockSpec((1, part, points), lambda i: (0, i, 0))
    wide = [iface + size, iface, size, size]
    latest, prior, *ends = call(
        bulk_kernel,
        [shape(1, rows, points)] * 2 + [shape(rows, w) for w in wide],
        cost=(2 * 2 * 3 * rows * points * size, 16 * rows * points),
        grid=(rows // part,),
        in_specs=[band, band, pl.BlockSpec(stiff.shape, lambda i: (0, 0, 0))],
        out_specs=[band, band] + [pl.BlockSpec((part, w), lambda i: (i, 0)) for w in wide],
    )(field, previous, stiff)

    if n > 8:
        got = [jnp.stack([got[arrival(n).index(k)] for k in range(n)])]
    summed, edges, ext = call(
        functools.partial(gather_kernel, n, iface, cap, rows, len(got)),
        [shape((n + 1) * rows, max(iface, chans)), shape(8, 2 * rows), shape(16, rows)],
        in_specs=[vmem] * len(got) + [anywhere] * (n_sub - 3) + [vmem],
        scratch_shapes=[pltpu.VMEM((n, 2 * rows, iface), BF16)],
    )(*got, prod, *tables[4:], table)
    crossed = lax.ppermute(summed, "grp", [(0, 1), (1, 0)])
    deep = -(-(n + 1) // 8) * 8
    height = 2 * rows * (iface // LANES) + 8
    part_shapes = [shape(height, LANES)] * n_sub
    high, low, hit, *begun = call(
        functools.partial(compact_kernel, n, n_sub, iface, cap, rows, len(got)),
        [shape(chans, chans, dtype=BF16)] * 2 + [shape(n, iface, iface, dtype=BF16)] + part_shapes,
        cost=LONG,
        scratch_shapes=[
            pltpu.VMEM((chans, 2 * iface), F32),
            pltpu.VMEM((deep, LANES), F32),
            pltpu.VMEM((deep, LANES), F32),
            pltpu.VMEM((deep, iface), F32),
        ],
    )(*got, summed, ext, prod, *tables)
    shares = call(
        functools.partial(share_kernel, n, n_sub, iface, cap, rows),
        part_shapes,
        scratch_shapes=[pltpu.VMEM((chans, iface), F32)],
    )(*got, crossed, high, low, hit, *begun)
    parts = [
        lax.ppermute(shares[k], ("grp", "sub"), [(i, i ^ (n_sub + k)) for i in range(2 * n_sub)])
        for k in range(n_sub - 1, -1, -1)
    ]

    return tuple(
        call(
            functools.partial(patch_kernel, n_sub, iface, rows),
            [shape(1, rows, points)] * 2,
            in_specs=[vmem] * (n_sub + 6) + [hbm] * 2,
            out_specs=[hbm] * 2,
            scratch_shapes=[
                pltpu.VMEM((rows, iface + size), F32),
                pltpu.VMEM((rows, iface), F32),
                pltpu.VMEM((rows, size), F32),
                pltpu.VMEM((rows, size), F32),
                pltpu.VMEM((chans, 1), F32),
                pltpu.SemaphoreType.DMA((4,)),
            ],
            input_output_aliases={n_sub + 6: 0, n_sub + 7: 1},
        )(*parts, edges, stiff, *ends, latest, prior)
    )


def solution(mesh):
    in_specs = (
        P("grp", "sub", "mer"),
        P("grp", "sub", "mer"),
        P("grp", None, None),
        P("grp", None, "sub"),
        P("grp", "mer", None),
        P("grp", "mer"),
        P("grp", "mer"),
    )
    out_specs = (P("grp", "sub", "mer"), P("grp", "sub", "mer"))
    return jax.shard_map(body, mesh=mesh, in_specs=in_specs, out_specs=out_specs, check_vma=False)
```

```python
import functools

import jax
import jax.numpy as jnp
from jax import lax
from jax.experimental import pallas as pl
from jax.experimental.pallas import tpu as pltpu
from jax.sharding import PartitionSpec as P

F32 = jnp.float32
BF16 = jnp.bfloat16
HIGHEST = lax.Precision.HIGHEST
VMEM_BYTES = 48 * 2**20
LANES = 128
LONG = (10**10, 10**6)
NT = (((1,), (1,)), ((), ()))


def split(x):
    high = x.astype(BF16)
    return high, (x - high.astype(F32)).astype(BF16)


def dot(a, b):
    return jnp.dot(a, b, preferred_element_type=F32)


def dot_nt(a, b):
    return lax.dot_general(a, b, NT, preferred_element_type=F32)


def times_matrix(x, matrix):
    rows, size = x.shape[0], matrix.shape[0]
    count = x.shape[1] // size
    tall = x if count == 1 else jnp.concatenate([x[:, e * size : (e + 1) * size] for e in range(count)], axis=0)
    high, low = split(tall)
    mh, ml = split(matrix)
    out = dot(high, mh) + (dot(low, mh) + dot(high, ml))
    if count == 1:
        return out
    return jnp.concatenate([out[e * rows : (e + 1) * rows] for e in range(count)], axis=1)


def neighbours(x):
    width = x.shape[1]
    col = lax.broadcasted_iota(jnp.int32, x.shape, 1)
    lower = jnp.where(col == 0, 0.0, pltpu.roll(x, 1, 1))
    higher = jnp.where(col == width - 1, 0.0, pltpu.roll(x, width - 1, 1))
    return lower + higher


def update(x, matrix):
    return 1.5 * x - 0.5 * times_matrix(x, matrix) + 0.25 * neighbours(x)


def layout(rows, iface, cap):
    cols, caps = iface // LANES, cap // LANES
    start = rows * (cols + caps)
    used = 2 * cols + caps + 2
    return cols, caps, start, start + -(-used // 8) * 8


def blocks(ref, start, rows, count):
    return jnp.concatenate([ref[start + j * rows : start + (j + 1) * rows, :] for j in range(count)], axis=1)


def strip_kernel(n, cap, field, previous, stiff, owner, face, weight, table, *refs):
    outs, copied = refs[:n], refs[n]
    wide_ref, fend_ref, prev_ref, pend_ref, stiff_ref, owner_ref, face_ref, weight_ref, chosen_ref, sems = refs[n + 1 :]
    rows, iface = prev_ref.shape
    size = fend_ref.shape[1]
    points = field.shape[2]
    pairs = [
        (owner, owner_ref),
        (face, face_ref),
        (weight, weight_ref),
        (stiff.at[0], stiff_ref),
        (field.at[0, :, pl.ds(0, iface + size)], wide_ref),
        (previous.at[0, :, pl.ds(0, iface)], prev_ref),
        (field.at[0, :, pl.ds(points - size, size)], fend_ref),
        (previous.at[0, :, pl.ds(points - size, size)], pend_ref),
        (table, copied),
    ]
    copies = [pltpu.make_async_copy(a, b, sems.at[i]) for i, (a, b) in enumerate(pairs)]
    for copy in copies:
        copy.start()
    me = lax.axis_index("mer")
    cols, caps, start, _ = layout(rows, iface, cap)
    count = -(-n // 8) * 8
    dest = lax.broadcasted_iota(jnp.int32, (count, iface), 0) ^ me
    before = lax.broadcasted_iota(jnp.int32, (iface, iface), 0) < lax.broadcasted_iota(jnp.int32, (iface, iface), 1)
    place = lax.broadcasted_iota(jnp.int32, (cap, iface), 0).astype(F32)
    for copy in copies[:3]:
        copy.wait()
    owners = owner_ref[...]
    weights = weight_ref[...]
    faces = face_ref[...].astype(F32)
    target = owners.astype(F32) * float(iface) + faces
    match = jnp.where(owners == dest, 1.0, 0.0)
    rank = dot(match.astype(BF16), jnp.where(before, 1.0, 0.0).astype(BF16))
    slots = jnp.where(match > 0.5, rank, -1.0)
    for k in range(n):
        chosen_ref[k] = jnp.where(slots[k : k + 1, :] == place, 1.0, 0.0).astype(BF16)
    for copy in copies[3:]:
        copy.wait()
    matrix = stiff_ref[...]
    wide = wide_ref[...]
    strip = wide[:, :iface]
    nxt = (1.5 * strip - prev_ref[...] - 0.5 * times_matrix(strip, matrix)) + 0.25 * neighbours(wide)[:, :iface]
    fend = fend_ref[...]
    nend = update(fend, matrix) - pend_ref[...]
    nh, nl = split(nxt * weights)
    fh, fl = split(jnp.concatenate([faces + 1.0, jnp.zeros((15, iface), F32)], axis=0))
    lhs = jnp.concatenate([nh, nl, fh, fl], axis=0)
    lasts = jnp.transpose(jnp.concatenate([fend, nend], axis=0))[size - 1 : size, :]
    firsts = jnp.transpose(jnp.concatenate([nxt[:, :size], strip[:, :size]], axis=0))[0:1, :]
    for k in range(n):
        out = outs[k]
        got = dot_nt(lhs, chosen_ref[k])
        picked = got[0:rows] + got[rows : 2 * rows]
        marks = got[2 * rows : 2 * rows + 1] + got[2 * rows + 16 : 2 * rows + 17] - 1.0
        for j in range(cols):
            span = slice(j * LANES, (j + 1) * LANES)
            out[j * rows : (j + 1) * rows, :] = strip[:, span]
            out[start + j : start + j + 1, :] = target[:, span]
            out[start + cols + j : start + cols + j + 1, :] = weights[:, span]
        for j in range(caps):
            span = slice(j * LANES, (j + 1) * LANES)
            out[(cols + j) * rows : (cols + j + 1) * rows, :] = picked[:, span]
            out[start + 2 * cols + j : start + 2 * cols + j + 1, :] = marks[:, span]
        out[start + 2 * cols + caps : start + 2 * cols + caps + 1, :] = lasts
        out[start + 2 * cols + caps + 1 : start + 2 * cols + caps + 2, :] = firsts


def bulk_kernel(field_ref, prev_ref, stiff_ref, latest_ref, prior_ref, llead_ref, plead_ref, ltail_ref, ptail_ref):
    matrix = stiff_ref[0]
    state = field_ref[0]
    first = update(state, matrix) - prev_ref[0]
    second = update(first, matrix) - state
    for value, whole, lead, tail in ((first, prior_ref, plead_ref, ptail_ref), (second, latest_ref, llead_ref, ltail_ref)):
        whole[0] = value
        lead[...] = value[:, : lead.shape[1]]
        tail[...] = value[:, value.shape[1] - tail.shape[1] :]


def packed(x):
    high = x.astype(BF16).astype(F32)
    low = x - high
    return jnp.transpose(jnp.concatenate([high, low, high], axis=0)).astype(BF16)


def tall(x):
    high, low = split(x)
    return jnp.concatenate([high, high, low], axis=0)


def synth_kernel(table_ref, prod_ref):
    prod_ref[...] = packed(table_ref[...])


def arrival(n):
    half = n // 2
    return [0, *([half] if half else []), *[k for k in range(1, n) if k != half]]


def message(refs, k):
    return refs[arrival(len(refs)).index(k)] if len(refs) > 1 else refs[0].at[k]


def loop(n, body, init):
    if n <= 8:
        for k in range(n):
            init = body(k, init)
        return init
    return lax.fori_loop(0, n, body, init)


def hits(target, base, iface):
    return jnp.where(target - base == lax.broadcasted_iota(jnp.int32, (iface, iface), 0).astype(F32), 1.0, 0.0).astype(BF16)


def domain_base(me, k, iface):
    return ((me ^ k) * iface).astype(F32)


def labels(ref, rows, iface, cap):
    cols, _, start, _ = layout(rows, iface, cap)
    row = lambda first: jnp.concatenate([ref[first + j : first + j + 1, :] for j in range(cols)], axis=1)
    return row(start), row(start + cols)


def edge_rows(ref, rows, iface, cap):
    cols, caps, start, _ = layout(rows, iface, cap)
    at = start + 2 * cols + caps
    return ref[at : at + 1, :], ref[at + 1 : at + 2, :]


def gather_kernel(n, iface, cap, rows, ks, count, *refs):
    msgs, (all_ref, edge_ref, ext_ref), store = refs[:count], refs[-4:-1], refs[-1]
    begun = refs[count : count + 3] if ks and 0 not in ks else None
    me = lax.axis_index("mer")
    beyond = ((me + 1) * iface).astype(F32)
    each = (lambda f, v: functools.reduce(lambda c, k: f(k, c), ks, v)) if ks else functools.partial(loop, n)
    at = (lambda k: msgs[ks.index(k)]) if ks else functools.partial(message, msgs)
    edge_ref[...] = begun[1][...] if begun else jnp.zeros(edge_ref.shape, F32)

    def one(k, ext):
        ref = at(k)
        target, weight = labels(ref, rows, iface, cap)
        both = jnp.concatenate(split(blocks(ref, 0, rows, iface // LANES) * weight), axis=0)
        store[k] = both
        mask = jnp.broadcast_to(jnp.where(target == beyond, 1.0, 0.0), (16, iface)).astype(BF16)
        ext = ext + dot_nt(mask, both[:rows]) + dot_nt(mask, both[rows:])
        last, first = edge_rows(ref, rows, iface, cap)
        edge_ref[0:1, :] += jnp.where((me ^ k) == me - 1, 1.0, 0.0) * last
        edge_ref[1:2, :] += jnp.where((me ^ k) == me + 1, 1.0, 0.0) * first
        return ext

    ext_ref[...] = each(one, begun[2][...] if begun else jnp.zeros((16, rows), F32))
    if not begun:
        last, first = edge_rows(at(0), rows, iface, cap)
        lane = lax.broadcasted_iota(jnp.int32, last.shape, 1)
        edge_ref[0:1, :] += jnp.where(lane >= rows, jnp.where(me > 0, 0.25, 0.0) * first, 0.0)
        edge_ref[1:2, :] += jnp.where(lane < rows, jnp.where(me < n - 1, 0.25, 0.0) * last, 0.0)

    def onto(j, carry):
        base = domain_base(me, j, iface)

        def add(k, total):
            return total + dot_nt(store[k], hits(labels(at(k), rows, iface, cap)[0], base, iface))

        total = each(add, jnp.zeros((2 * rows, iface), F32))
        where = (pl.ds(j * rows, rows), slice(0, iface))
        value = total[:rows] + total[rows:]
        all_ref[where] = value + begun[0][where] if begun else value
        return carry

    loop(n, onto, 0)
    if not ks or begun:
        table_ref = refs[-5]
        all_ref[n * rows :, 0 : table_ref.shape[1]] = table_ref[...]


def compact_kernel(n, n_sub, iface, cap, rows, count, *refs):
    msgs, (zown_ref, ext_ref, prod_ref, table_ref, hit_ref, *outs) = refs[:count], refs[count:-4]
    force_ref = refs[-4]
    sub = lax.axis_index("sub")
    lasts, values, marks = refs[-3:]
    me = lax.axis_index("mer")
    cols, caps, start, _ = layout(rows, iface, cap)
    base = (me * iface).astype(F32)
    lasts[...] = jnp.zeros(lasts.shape, F32)
    values[...] = jnp.zeros(values.shape, F32)
    marks[...] = jnp.zeros(marks.shape, F32)
    face = lax.broadcasted_iota(jnp.int32, (iface, LANES), 0).astype(F32)
    line = lax.broadcasted_iota(jnp.int32, (1, iface), 1).astype(F32)

    def keep(k, carry):
        lasts[pl.ds((me ^ k) + 1, 1), :] = edge_rows(message(msgs, k), rows, iface, cap)[0]
        return carry

    loop(n, keep, 0)

    def one(k, total):
        ref = message(msgs, k)
        for j in range(caps):
            both = jnp.concatenate(split(ref[(cols + j) * rows : (cols + j + 1) * rows, :]), axis=0)
            marked = ref[start + 2 * cols + j : start + 2 * cols + j + 1, :]
            total = total + dot_nt(both, jnp.where(marked == face, 1.0, 0.0).astype(BF16))
        values[pl.ds(k, 1), :] = lasts[pl.ds(me ^ k, 1), :]
        target = ref[start : start + 1, 0:1] - base
        weight = 0.25 * ref[start + cols : start + cols + 1, 0:1]
        marks[pl.ds(k, 1), :] = jnp.where(target == line, weight, 0.0)
        hit_ref[k] = hits(labels(ref, rows, iface, cap)[0], base, iface)
        return total

    total = loop(n, one, jnp.zeros((2 * rows, iface), F32))
    first = jnp.dot(jnp.transpose(values[...]), marks[...], precision=HIGHEST, preferred_element_type=F32)
    prod = prod_ref[...]
    force_ref[:, 0:iface] = dot(prod, tall(zown_ref[0:rows, 0:iface]))
    force_ref[:, iface:] = dot(prod, tall(total[:rows] + total[rows:] + first[:rows]))
    ext = jnp.dot(ext_ref[0:8], table_ref[...], precision=HIGHEST, preferred_element_type=F32)
    for k in range(n_sub):
        where = pl.ds(pl.multiple_of((sub ^ k) * rows, rows), rows)
        for j in range(2 * cols):
            outs[k][j * rows : (j + 1) * rows, :] = force_ref[where, j * LANES : (j + 1) * LANES]
        for j in range(ext.shape[1] // LANES):
            at = 2 * cols * rows + j
            outs[k][at : at + 1, :] = ext[0:1, j * LANES : (j + 1) * LANES]


def operator_kernel(n_sub, rows, *refs):
    tables, (high_ref, low_ref) = refs[:n_sub], refs[-2:]
    for k in range(n_sub):
        where = pl.ds(pl.multiple_of((lax.axis_index("sub") ^ k) * rows, rows), rows)
        high_ref[where, :], low_ref[where, :] = split(tables[k][...])


def share_kernel(n, n_sub, iface, cap, rows, *refs):
    msgs, (zother_ref, high_ref, low_ref, hit_ref) = refs[: -2 * n_sub - 5], refs[-2 * n_sub - 5 : -2 * n_sub - 1]
    begun, outs, more_ref = refs[-2 * n_sub - 1 : -n_sub - 1], refs[-n_sub - 1 : -1], refs[-1]
    sub = lax.axis_index("sub")
    cols = iface // LANES
    high, low = split(0.5 * zother_ref[n * rows :, 0 : high_ref.shape[1]])
    double = packed(dot(high, high_ref[...]) + (dot(low, high_ref[...]) + dot(high, low_ref[...])))

    def add(k, total):
        weight = labels(message(msgs, k), rows, iface, cap)[1]
        both = jnp.concatenate(split(zother_ref[pl.ds(k * rows, rows), 0:iface] * weight), axis=0)
        return total + dot_nt(both, hit_ref[k])

    total = loop(n, add, jnp.zeros((2 * rows, iface), F32))
    more_ref[...] = dot(double, tall(total[:rows] + total[rows:]))
    for k in range(n_sub):
        where = pl.ds(pl.multiple_of((sub ^ k) * rows, rows), rows)
        outs[k][: cols * rows, :] = begun[k][: cols * rows, :]
        outs[k][2 * cols * rows :, :] = begun[k][2 * cols * rows :, :]
        for j in range(cols):
            span = slice((cols + j) * rows, (cols + j + 1) * rows)
            outs[k][span, :] = begun[k][span, :] + more_ref[where, j * LANES : (j + 1) * LANES]


def patch_kernel(n_sub, iface, rows, *refs):
    parts = refs[:n_sub]
    edge_ref, stiff_ref, llead, plead, ltail, ptail, _, _, latest_ref, prior_ref = refs[n_sub : n_sub + 10]
    lbuf, pbuf, lend, pend, turned, sems = refs[n_sub + 10 :]
    sub = lax.axis_index("sub")
    matrix = stiff_ref[0]
    size = matrix.shape[0]
    points = latest_ref.shape[2]
    cols = iface // LANES
    edges = jnp.transpose(edge_ref[...])

    def push(i, buf, out, start):
        copy = pltpu.make_async_copy(buf, out.at[0, :, pl.ds(start, buf.shape[1])], sems.at[i])
        copy.start()
        return copy

    total = functools.reduce(lambda a, b: a + b, [p[...] for p in parts])
    pick = lambda first: jnp.concatenate([total[(first + j) * rows : (first + j + 1) * rows] for j in range(cols)], axis=1)
    force, force1 = pick(0), pick(cols)
    col = lax.broadcasted_iota(jnp.int32, (rows, iface), 1)
    delta = 0.5 * force + jnp.where(col == 0, 0.25 * edges[0:rows, 0:1], 0.0)
    pbuf[...] = plead[...] + delta
    copies = [push(0, pbuf, prior_ref, 0)]
    end = lax.broadcasted_iota(jnp.int32, (rows, size), 1)
    change = update(delta, matrix) + 0.5 * force1 + jnp.where(col == 0, 0.25 * edges[rows : 2 * rows, 0:1], 0.0)
    lbuf[:, 0:iface] = llead[:, 0:iface] + change
    lbuf[:, iface:] = llead[:, iface:] + jnp.where(end == 0, 0.25 * delta[:, iface - 1 : iface], 0.0)
    copies.append(push(3, lbuf, latest_ref, 0))
    shift = jnp.where(end == size - 1, 0.25 * edges[rows : 2 * rows, 1:2], 0.0)
    pend[...] = ptail[...] + shift
    copies.append(push(1, pend, prior_ref, points - size))
    ext = jnp.transpose(total[2 * cols * rows :])
    for j in range(turned.shape[0] // LANES):
        turned[j * LANES : (j + 1) * LANES, :] = ext[:, j : j + 1]
    beyond = edges[0:rows, 1:2] + 0.5 * turned[pl.ds(pl.multiple_of(sub * rows, rows), rows), :]
    lend[...] = ltail[...] + update(shift, matrix) + jnp.where(end == size - 1, 0.25 * beyond, 0.0)
    copies.append(push(2, lend, latest_ref, points - size))
    for copy in copies:
        copy.wait()


def call(kernel, outs, cost=None, vmem=VMEM_BYTES, **more):
    params = pltpu.CompilerParams(vmem_limit_bytes=vmem)
    estimate = None if cost is None else pl.CostEstimate(flops=cost[0], bytes_accessed=cost[1], transcendentals=0)
    return pl.pallas_call(kernel, out_shape=outs, compiler_params=params, cost_estimate=estimate, **more)


def shape(*dims, dtype=F32):
    return jax.ShapeDtypeStruct(dims, dtype)


def body(field, previous, stiff, synth, owner, face, weight):
    n, n_sub = lax.axis_size("mer"), lax.axis_size("sub")
    _, rows, points = field.shape
    size = stiff.shape[1]
    iface = face.shape[1]
    chans = synth.shape[1]
    cap = -(-(2 * iface // n) // LANES) * LANES
    depth = layout(rows, iface, cap)[3]
    hbm = pl.BlockSpec(memory_space=pltpu.HBM)
    anywhere = pl.BlockSpec(memory_space=pl.ANY)
    vmem = pl.BlockSpec(memory_space=pltpu.VMEM)

    *msgs, table = call(
        functools.partial(strip_kernel, n, cap),
        [shape(depth, LANES)] * n + [shape(rows, chans)],
        in_specs=[hbm] * 7,
        out_specs=[vmem] * (n + 1),
        scratch_shapes=[
            pltpu.VMEM((rows, iface + size), F32),
            pltpu.VMEM((rows, size), F32),
            pltpu.VMEM((rows, iface), F32),
            pltpu.VMEM((rows, size), F32),
            pltpu.VMEM((size, size), F32),
            pltpu.VMEM((1, iface), jnp.int32),
            pltpu.VMEM((1, iface), jnp.int32),
            pltpu.VMEM((1, iface), F32),
            pltpu.VMEM((n, cap, iface), BF16),
            pltpu.SemaphoreType.DMA((9,)),
        ],
    )(*[pltpu.with_memory_space_constraint(v, pltpu.HBM) for v in (field, previous, stiff, owner.reshape(1, iface), face, weight, jnp.transpose(synth[0]))])

    got = [msgs[0]] + [lax.ppermute(msgs[k], "mer", [(i, i ^ k) for i in range(n)]) for k in arrival(n)[1:]]

    tables = [table] + [lax.ppermute(table, "sub", [(i, i ^ k) for i in range(n_sub)]) for k in range(1, n_sub)]
    prod = call(synth_kernel, shape(chans, 3 * rows, dtype=BF16))(table)

    part = 16
    band = pl.BlockSpec((1, part, points), lambda i: (0, i, 0))
    wide = [iface + size, iface, size, size]
    latest, prior, *ends = call(
        bulk_kernel,
        [shape(1, rows, points)] * 2 + [shape(rows, w) for w in wide],
        cost=(2 * 2 * 3 * rows * points * size, 16 * rows * points),
        grid=(rows // part,),
        in_specs=[band, band, pl.BlockSpec(stiff.shape, lambda i: (0, 0, 0))],
        out_specs=[band, band] + [pl.BlockSpec((part, w), lambda i: (i, 0)) for w in wide],
    )(field, previous, stiff)

    if n > 8:
        got = [jnp.stack([got[arrival(n).index(k)] for k in range(n)])]
    order = arrival(n)
    begun = []
    for ks in [tuple(order[:-1]), (order[-1],)] if 1 < n <= 8 else [()]:
        values = [got[order.index(k)] for k in ks] or got
        last = [prod, table] if not ks or begun else []
        begun = call(
            functools.partial(gather_kernel, n, iface, cap, rows, ks, len(values)),
            [shape((n + 1) * rows, max(iface, chans)), shape(8, 2 * rows), shape(16, rows)],
            in_specs=[vmem] * (len(values) + len(begun)) + [anywhere, vmem] * bool(last),
            scratch_shapes=[pltpu.VMEM((n, 2 * rows, iface), BF16)],
        )(*values, *begun, *last)
    summed, edges, ext = begun
    crossed = lax.ppermute(summed, "grp", [(0, 1), (1, 0)])
    deep = -(-(n + 1) // 8) * 8
    height = 2 * rows * (iface // LANES) + 8
    part_shapes = [shape(height, LANES)] * n_sub
    hit, *begun = call(
        functools.partial(compact_kernel, n, n_sub, iface, cap, rows, len(got)),
        [shape(n, iface, iface, dtype=BF16)] + part_shapes,
        scratch_shapes=[
            pltpu.VMEM((chans, 2 * iface), F32),
            pltpu.VMEM((deep, LANES), F32),
            pltpu.VMEM((deep, LANES), F32),
            pltpu.VMEM((deep, iface), F32),
        ],
    )(*got, summed, ext, prod, table)
    high, low = call(
        functools.partial(operator_kernel, n_sub, rows),
        [shape(chans, chans, dtype=BF16)] * 2,
        cost=LONG,
        in_specs=[vmem] * n_sub + [anywhere],
    )(*tables, hit)
    shares = call(
        functools.partial(share_kernel, n, n_sub, iface, cap, rows),
        part_shapes,
        scratch_shapes=[pltpu.VMEM((chans, iface), F32)],
    )(*got, crossed, high, low, hit, *begun)
    parts = [
        lax.ppermute(shares[k], ("grp", "sub"), [(i, i ^ (n_sub + k)) for i in range(2 * n_sub)])
        for k in range(n_sub - 1, -1, -1)
    ]

    return tuple(
        call(
            functools.partial(patch_kernel, n_sub, iface, rows),
            [shape(1, rows, points)] * 2,
            in_specs=[vmem] * (n_sub + 6) + [hbm] * 2,
            out_specs=[hbm] * 2,
            scratch_shapes=[
                pltpu.VMEM((rows, iface + size), F32),
                pltpu.VMEM((rows, iface), F32),
                pltpu.VMEM((rows, size), F32),
                pltpu.VMEM((rows, size), F32),
                pltpu.VMEM((chans, 1), F32),
                pltpu.SemaphoreType.DMA((4,)),
            ],
            input_output_aliases={n_sub + 6: 0, n_sub + 7: 1},
        )(*parts, edges, stiff, *ends, latest, prior)
    )


def solution(mesh):
    in_specs = (
        P("grp", "sub", "mer"),
        P("grp", "sub", "mer"),
        P("grp", None, None),
        P("grp", None, "sub"),
        P("grp", "mer", None),
        P("grp", "mer"),
        P("grp", "mer"),
    )
    out_specs = (P("grp", "sub", "mer"), P("grp", "sub", "mer"))
    return jax.shard_map(body, mesh=mesh, in_specs=in_specs, out_specs=out_specs, check_vma=False)
```
